512 devices in a mesh: px: 64 (over y, z_hi, x, core), pz: 8 (over z_lo).
Axes of the slice: x: 4, y: 4, z: 16 (z_hi: 2, z_lo: 8; z = z_hi * 8 + z_lo), core: 2. Of those that a mesh axis runs over, the one named last changes fastest.
Arguments:
- wall_vel: bfloat16 [512, 512, 192], P('pz', 'px'), may hold values from -1.1953125 to 1.1953125
- wall_slope: bfloat16 [512, 512, 192], P('pz', 'px'), may hold values from -600 to 600
- wall_curvature: bfloat16 [512, 512, 192], P('pz', 'px'), may hold values from -600 to 600
- vorticity: bfloat16 [512, 512, 192], P('pz', 'px'), may hold values from -6 to 6
- vort_slope: bfloat16 [512, 512, 192], P('pz', 'px'), may hold values from -60 to 60
- mean_profile: float32 [4, 192], replicated, may hold values from -1200 to 1200
- eigen_basis: bfloat16 [192, 192], replicated, as said below
- eigen_decay: float32 [192], replicated, may hold values from 0 to 4, as said below
- viscous_step: float32 [1], replicated, may hold values from 0.0001 to 0.0004
- time_step: float32 [1], replicated, may hold values from 0.01 to 0.03
Outputs:
- vorticity_next: bfloat16 [512, 512, 192], P('pz', 'px')
The draws below stay inside these ranges and needn't reach their ends.
Inputs may be any that keep to these rules, and one draw needn't show every extreme that they name: `eigen_basis`: the columns are orthonormal eigenvectors of the second difference over 192 points with zero wall values, in some order and with some signs, rounded. `eigen_decay`: one positive factor times the eigenvalue magnitude of the matching column of eigen_basis.
All inputs are finite; a program needn't handle non-finite values.
Results may differ from the reference program's by a relative error of at most 0.011.
Values may be sent and summed in bfloat16 or wider, within the bound.
A program may use at most 128 MiB of HBM per device.

```python
import math
import jax
import jax.numpy as jnp
from jax import lax

NKX = 512
NKZ = 512
NY = 192
NXP = 768
NZP = 768


def eigen_order(key):
    order = jax.random.permutation(key, NY).astype(jnp.int32)
    signs = (jax.random.randint(jax.random.fold_in(key, 11), (NY,), 0, 2) * 2 - 1).astype(jnp.float32)
    return (order, signs)


def draw_eigen_basis(key, part):
    order, signs = eigen_order(key)
    points = jnp.arange(NY, dtype=jnp.int32) + 1
    phase = points[:, None] * (order[None, :] + 1) % (2 * (NY + 1))
    angles = phase.astype(jnp.float32) * (math.pi / (NY + 1))
    basis = math.sqrt(2.0 / (NY + 1)) * jnp.sin(angles) * signs[None, :]
    return basis.astype(jnp.bfloat16)


def draw_eigen_decay(key, part):
    order, signs = eigen_order(key)
    key = jax.random.fold_in(key, 5)
    strength = jax.random.uniform(key, (), jnp.float32, 0.5, 1.0)
    angles = (order + 1).astype(jnp.float32) * (math.pi / (NY + 1))
    return (strength * 2.0 * (1.0 - jnp.cos(angles))).astype(jnp.float32)


def steps_of(own_key, extent, pieces, low, largest):
    def one(position, blocks):
        steps = jax.random.uniform(jax.random.fold_in(jax.random.fold_in(own_key, 6), position), (blocks,), jnp.float32, low / len(pieces), largest / len(pieces))
        return jnp.repeat(jnp.exp(steps), extent[position] // blocks).reshape((-1,) + (1,) * (len(extent) - position - 1))

    level = one(*pieces[0])
    for cut in pieces[1:]:
        level = level * one(*cut)
    return level


def bell_draw(stream_key, extent, scale, reach, shards=(), held_as=jnp.bfloat16):
    result = scale * jax.random.normal(stream_key, extent, jnp.float32)
    if shards:
        result = result * steps_of(stream_key, extent, shards, -0.22, 0.18)
    return jnp.clip(result, -reach, reach).astype(held_as)


def setup_inputs(seed: int = 0) -> dict:
    arg_keys = jax.random.split(jax.random.key(seed), 11)
    return {
        "wall_vel": bell_draw(arg_keys[0], (NKZ, NKX, NY), 0.2, 1.1953125, ((0, 8), (1, 64))),
        "wall_slope": bell_draw(arg_keys[1], (NKZ, NKX, NY), 100.0, 600.0, ((0, 8), (1, 64))),
        "wall_curvature": bell_draw(arg_keys[2], (NKZ, NKX, NY), 100.0, 600.0, ((0, 8), (1, 64))),
        "vorticity": bell_draw(arg_keys[3], (NKZ, NKX, NY), 1.0, 6.0, ((0, 8), (1, 64))),
        "vort_slope": bell_draw(arg_keys[4], (NKZ, NKX, NY), 10.0, 60.0, ((0, 8), (1, 64))),
        "mean_profile": bell_draw(arg_keys[5], (4, NY), 200.0, 1200.0, (), jnp.float32),
        "eigen_basis": draw_eigen_basis(jax.random.fold_in(arg_keys[10], 71), 0),
        "eigen_decay": draw_eigen_decay(jax.random.fold_in(arg_keys[10], 71), 0),
        "viscous_step": jnp.clip(jax.random.uniform(arg_keys[8], (1,), jnp.float32, 0.0001, 0.0004), 0.0001, 0.0004),
        "time_step": jnp.clip(jax.random.uniform(arg_keys[9], (1,), jnp.float32, 0.01, 0.03), 0.01, 0.03),
    }


STREAM_SCALE = 0.25
SPAN_SCALE = 2.0 / 3.0
EXPLICIT = 29.0 / 96.0
IMPLICIT = 37.0 / 160.0
FORCING = 8.0 / 15.0

def make_tables(count, points, scale):
    indices = jnp.arange(count, dtype=jnp.int32)
    number = indices // 2
    cosine = (indices % 2 == 0)[:, None]
    grid = jnp.arange(points, dtype=jnp.int32)
    phase = number[:, None] * grid[None, :] % points
    angles = phase.astype(jnp.float32) * (2.0 * math.pi / points)
    cos_part = jnp.cos(angles)
    sin_part = jnp.sin(angles)
    shape_rows = jnp.where(cosine, cos_part, sin_part)
    norm = math.sqrt(2.0 / count)
    synthesis = (norm * shape_rows).astype(jnp.bfloat16)
    analysis = (2.0 / points / norm * shape_rows).T.astype(jnp.bfloat16)
    slope_rows = jnp.where(cosine, sin_part, -cos_part)
    factor = (scale * number.astype(jnp.float32))[:, None] * (2.0 / points / norm)
    slope_analysis = (factor * slope_rows).T.astype(jnp.bfloat16)
    return (synthesis, analysis, slope_analysis)

def wave_rates(count, start, scale):
    indices = jnp.arange(count, dtype=jnp.int32) + start
    return scale * (indices // 2).astype(jnp.float32)

def pair_turn(field, dim, rates):
    shape = field.shape
    size = shape[dim]
    split = shape[:dim] + (size // 2, 2) + shape[dim + 1:]
    swapped = jnp.flip(field.reshape(split), axis=dim + 1).reshape(shape)
    parity = jnp.arange(size, dtype=jnp.int32) % 2
    factor = jnp.where(parity == 0, 1.0, -1.0).astype(jnp.float32) * rates
    view = [1] * len(shape)
    view[dim] = size
    return swapped * factor.reshape(view)

def reference(wall_vel, wall_slope, wall_curvature, vorticity, vort_slope, mean_profile, eigen_basis, eigen_decay, viscous_step, time_step):
    syn_x, ana_x, slope_x = make_tables(NKX, NXP, STREAM_SCALE)
    syn_z, ana_z, slope_z = make_tables(NKZ, NZP, SPAN_SCALE)
    kx_rates = wave_rates(NKX, 0, STREAM_SCALE)
    kz_rates = wave_rates(NKZ, 0, SPAN_SCALE)
    wave_square = kz_rates[:, None] ** 2 + kx_rates[None, :] ** 2
    safe_square = jnp.where(wave_square == 0.0, 1.0, wave_square)
    corner = ((jnp.arange(NKZ) == 0)[:, None] & (jnp.arange(NKX) == 0)[None, :]).astype(jnp.float32)
    f32 = jnp.float32

    def planes(field):
        return jnp.transpose(field, (2, 0, 1)).reshape(NY // 8, 8, NKZ, NKX)
    mean_planes = jnp.transpose(mean_profile.reshape(4, NY // 8, 8), (1, 0, 2))

    def plane_block(group):
        vel_b, slope_b, curv_b, vort_b, vslope_b, means = group
        sv = slope_b.astype(f32) / safe_square
        cv = curv_b.astype(f32) / safe_square
        ov = vort_b.astype(f32) / safe_square
        qv = vslope_b.astype(f32) / safe_square
        vel32 = vel_b.astype(f32)
        lift = corner[None]
        stream_vel = pair_turn(sv, 2, kx_rates) - pair_turn(ov, 1, kz_rates) + lift * means[0][:, None, None]
        span_vel = pair_turn(sv, 1, kz_rates) + pair_turn(ov, 2, kx_rates) + lift * means[1][:, None, None]
        stream_vort = pair_turn(cv, 1, kz_rates) + pair_turn(qv, 2, kx_rates) - pair_turn(vel32, 1, kz_rates) + lift * means[3][:, None, None]
        span_vort = pair_turn(vel32, 2, kx_rates) - pair_turn(cv, 2, kx_rates) + pair_turn(qv, 1, kz_rates) - lift * means[2][:, None, None]
        fields = jnp.stack([stream_vel, span_vel, vel32, stream_vort, vort_b.astype(f32), span_vort]).astype(jnp.bfloat16)
        span_grid = jnp.einsum('fykx,kp->fypx', fields.astype(f32), syn_z.astype(f32)).astype(jnp.bfloat16)
        grid = jnp.einsum('fypx,xq->fypq', span_grid.astype(f32), syn_x.astype(f32))
        flux_stream = (grid[0] * grid[4] - grid[2] * grid[3]).astype(jnp.bfloat16)
        flux_span = (grid[1] * grid[4] - grid[2] * grid[5]).astype(jnp.bfloat16)
        stream_part = jnp.einsum('ypq,qx->ypx', flux_stream.astype(f32), slope_x.astype(f32)).astype(jnp.bfloat16)
        span_part = jnp.einsum('ypq,qx->ypx', flux_span.astype(f32), ana_x.astype(f32)).astype(jnp.bfloat16)
        total = jnp.einsum('ypx,pk->ykx', stream_part.astype(f32), ana_z.astype(f32))
        total = total + jnp.einsum('ypx,pk->ykx', span_part.astype(f32), slope_z.astype(f32))
        return (-total).astype(jnp.bfloat16)
    nonlinear = lax.map(plane_block, (planes(wall_vel), planes(wall_slope), planes(wall_curvature), planes(vorticity), planes(vort_slope), mean_planes))
    nonlinear = jnp.transpose(nonlinear.reshape(NY, NKZ, NKX), (1, 2, 0))

    def solve_row(triple):
        vort_rows, flux_rows, kz_value = triple
        square = (kz_value * kz_value + kx_rates * kx_rates)[:, None]
        rates = eigen_decay[None, :] + viscous_step[0] * square
        old_coef = jnp.dot(vort_rows, eigen_basis, preferred_element_type=jnp.float32)
        flux_coef = jnp.dot(flux_rows, eigen_basis, preferred_element_type=jnp.float32)
        denom = 1.0 + IMPLICIT * rates
        mixed = ((1.0 - EXPLICIT * rates) / denom * old_coef + FORCING * time_step[0] / denom * flux_coef).astype(jnp.bfloat16)
        return jnp.dot(mixed, eigen_basis.T, preferred_element_type=jnp.float32).astype(jnp.bfloat16)
    return lax.map(solve_row, (vorticity, nonlinear, kz_rates))
```

```python
import functools
import math

import jax
import jax.numpy as jnp
import ml_dtypes
import numpy as np
from jax import lax
from jax.experimental import pallas as pl
from jax.experimental.pallas import tpu as pltpu
from jax.sharding import PartitionSpec as P

NR = 8
WALLS = 3
FIELDS = 5
QUADS = 4
KZB = 64
KXB = 8

STREAM_SCALE = 0.25
SPAN_SCALE = 2.0 / 3.0
EXPLICIT = 29.0 / 96.0
IMPLICIT = 37.0 / 160.0
FORCING = 8.0 / 15.0

BF = jnp.bfloat16
F32 = jnp.float32

SLOPE, CURV, VORT, VSLOPE, VEL = range(FIELDS)


def make_tables(count, points, scale):
    indices = np.arange(count)
    number = indices // 2
    cosine = (indices % 2 == 0)[:, None]
    phase = number[:, None] * np.arange(points)[None, :] % points
    angles = phase * (2.0 * math.pi / points)
    cos_part, sin_part = np.cos(angles), np.sin(angles)
    shape_rows = np.where(cosine, cos_part, sin_part)
    norm = math.sqrt(2.0 / count)
    synthesis = norm * shape_rows
    analysis = (2.0 / points / norm * shape_rows).T
    slope_rows = np.where(cosine, sin_part, -cos_part)
    slope_analysis = ((scale * number)[:, None] * (2.0 / points / norm) * slope_rows).T

    def rounded(t):
        return t.astype(np.float32).astype(ml_dtypes.bfloat16)

    return rounded(synthesis), rounded(analysis), rounded(slope_analysis)


def all_tables(ng, nr, npz):
    kxb = KXB * ng
    nkx, nkz = kxb * nr, KZB * npz
    syn_x, ana_x, slope_x = make_tables(nkx, nkx * 3 // 2, STREAM_SCALE)
    syn_z, ana_z, slope_z = make_tables(nkz, nkz * 3 // 2, SPAN_SCALE)
    r, c, m, g = np.meshgrid(
        np.arange(nr), np.arange(QUADS), np.arange(2), np.arange(ng), indexing="ij"
    )
    order = (g * (KXB * nr) + r * KXB + 2 * c + m).reshape(nr, kxb)
    plain = order.reshape(-1)
    crossed = order.reshape(nr // 2, 2, kxb)[:, ::-1].reshape(-1)
    rows = KZB * KXB
    move = np.zeros((rows, rows), np.float32)
    kz, kx = np.meshgrid(np.arange(KZB), np.arange(KXB), indexing="ij")
    move[(kz * KXB + kx).reshape(-1), (kx * KZB + kz).reshape(-1)] = 1.0
    return (
        move.astype(ml_dtypes.bfloat16),
        np.ascontiguousarray(syn_z.T),
        np.ascontiguousarray(syn_x[plain]),
        np.ascontiguousarray(syn_x[crossed]),
        np.ascontiguousarray(slope_x[:, plain]),
        np.ascontiguousarray(ana_x[:, crossed]),
        ana_z,
        slope_z,
    )


def dot(a, b, ca, cb):
    return lax.dot_general(a, b, (((ca,), (cb,)), ((), ())), preferred_element_type=F32)


def kernel_body(
    ng, nr, npz,
    slope_h, curv_h, vort_h, vslope_h, vel_h,
    move_h, synz_h, synx0_h, synx1_h, slopex_h, anax_h, anaz_h, slopez_h,
    mean_ref, basis_ref, decay_ref, visc_ref, dt_ref,
    out_ref,
    xin, move, synz, synx0, synx1, slopex, anax, anaz, slopez,
    stage, send_a, recv_a, wide, coef, mixed_rows, send_b, recv_b, lhs, flux,
    send_c, recv_c, back, send_d, recv_d, old, spread,
    in_sem, tab_sem, own_sem, sa_sem, ra_sem, sb_sem, rb_sem, sc_sem, rc_sem, sd_sem, rd_sem,
):
    owners = ng * npz
    kxl = KXB * ng
    zb = synz.shape[0] // nr
    px = lax.axis_index("px")
    pz = lax.axis_index("pz")
    g = px // nr
    r = px % nr
    me = pz * ng + g
    par = r % 2

    def owner(s):
        return {"px": (s % ng) * nr + r, "pz": s // ng}

    def peer(q):
        return {"px": g * nr + q, "pz": pz}

    ins = [
        pltpu.make_async_copy(h, xin.at[i], in_sem.at[i])
        for i, h in enumerate((slope_h, curv_h, vort_h, vslope_h, vel_h))
    ]
    tabs = [
        pltpu.make_async_copy(h, v, tab_sem.at[i])
        for i, (h, v) in enumerate(
            (
                (move_h, move), (synz_h, synz), (synx0_h, synx0), (synx1_h, synx1),
                (slopex_h, slopex), (anax_h, anax), (anaz_h, anaz), (slopez_h, slopez),
            )
        )
    ]
    tabs[0].start()
    for copy in ins:
        copy.start()
    for copy in tabs[1:]:
        copy.start()

    barrier = pltpu.get_barrier_semaphore()

    @pl.loop(1, owners)
    def _(t):
        pl.semaphore_signal(
            barrier, inc=1, device_id=owner((me + t) % owners),
            device_id_type=pl.DeviceIdType.MESH,
        )

    @pl.loop(1, nr)
    def _(t):
        pl.semaphore_signal(
            barrier, inc=1, device_id=peer((r + t) % nr),
            device_id_type=pl.DeviceIdType.MESH,
        )

    tabs[0].wait()
    per_owner = FIELDS * QUADS
    for i in range(FIELDS):
        ins[i].wait()
        block = xin[i].reshape(KZB * KXB, xin.shape[3])
        turned = dot(block, move[...], 0, 0)
        for j in range(WALLS):
            for c in range(QUADS):
                stage[pl.ds(j * owners * per_owner + i * QUADS + c, owners, stride=per_owner), :] = (
                    turned[j * owners : (j + 1) * owners, 128 * c : 128 * c + 128]
                )
        if i == VORT:
            old[...] = dot(basis_ref[...], turned.astype(BF), 0, 0)

    for j in range(WALLS):
        rows = owners * per_owner
        send_a[j] = (
            stage[j * rows : (j + 1) * rows, :].astype(BF).reshape(owners, FIELDS, QUADS, 128)
        )

    pl.semaphore_wait(barrier, owners - 1 + nr - 1)

    for j in range(WALLS):
        pltpu.make_async_copy(send_a.at[j, me], recv_a.at[j, me], ra_sem.at[j]).start()

        @pl.loop(1, owners)
        def _(t, j=j):
            to = (me + t) % owners
            pltpu.make_async_remote_copy(
                src_ref=send_a.at[j, to], dst_ref=recv_a.at[j, me],
                send_sem=sa_sem.at[j], recv_sem=ra_sem.at[j],
                device_id=owner(to), device_id_type=pl.DeviceIdType.MESH,
            ).start()

    row = lax.broadcasted_iota(jnp.int32, (owners, 128), 0)
    lane = lax.broadcasted_iota(jnp.int32, (owners, 128), 1)
    lower = lane < KZB
    even = lane % 2 == 0
    kz_rate = SPAN_SCALE * ((KZB // 2) * (row // ng) + (lane % KZB) // 2).astype(F32)
    fz = jnp.where(even, kz_rate, -kz_rate)
    for c in range(QUADS):
        number = (KXB // 2) * nr * (row % ng) + (KXB // 2) * r + c
        kx_rate = STREAM_SCALE * number.astype(F32)
        fx = jnp.where(lower, kx_rate, -kx_rate)
        square = kx_rate * kx_rate + kz_rate * kz_rate
        safe = jnp.where(square == 0.0, 1.0, square)
        coef[c, 0] = fx
        coef[c, 1] = fx / safe
        coef[c, 2] = fz / safe
    coef[0, 3] = fz

    points = basis_ref.shape[0]
    col = lax.broadcasted_iota(jnp.int32, (points, points * QUADS), 1)
    point = lax.broadcasted_iota(jnp.int32, (points, points * QUADS), 0)
    wide_basis = dot(
        basis_ref[...], jnp.where(col // QUADS == point, 1.0, 0.0).astype(BF), 0, 0
    )
    for c in range(QUADS):
        spread[c * points : (c + 1) * points, :] = jnp.where(
            col % QUADS == c, wide_basis, 0.0
        ).astype(BF)

    def swap_x(v):
        return pltpu.roll(v, KZB, 1)

    def swap_z(v):
        return jnp.where(even, pltpu.roll(v, 127, 1), pltpu.roll(v, 1, 1))

    first = (row == 0) & (lane == 0) & (px == g * nr) & (r == 0)

    def forward(j):
        pltpu.make_async_copy(recv_a.at[j], recv_a.at[j], ra_sem.at[j]).wait()
        wide[...] = recv_a[j].reshape(owners * per_owner, 128).astype(F32)
        if j == 0:
            tabs[1].wait()
        for c in range(QUADS):
            def load(i, c=c):
                return wide[pl.ds(i * QUADS + c, owners, stride=per_owner), :]

            s, cv, o, q, v = (load(i) for i in range(FIELDS))
            fx, a, b, fzz = coef[c, 0], coef[c, 1], coef[c, 2], coef[0, 3]
            stream_vel = swap_z(b * o) - swap_x(a * s)
            span_vel = -swap_z(b * s) - swap_x(a * o)
            stream_vort = swap_z(fzz * v - b * cv) - swap_x(a * q)
            span_vort = swap_x(a * cv - fx * v) - swap_z(b * q)
            if c == 0:
                def mean(i):
                    return jnp.where(first, mean_ref[i, owners * j + me], 0.0)

                stream_vel += mean(0)
                span_vel += mean(1)
                stream_vort += mean(3)
                span_vort -= mean(2)
            for f, field in enumerate((stream_vel, span_vel, v, stream_vort, o, span_vort)):
                at = pl.multiple_of((f + par - 2 * par * (f % 2)) * kxl + c * 2 * ng, 2 * ng)
                low, high = [], []
                for p in range(npz // 2):
                    one = field[2 * p * ng : (2 * p + 1) * ng]
                    two = field[(2 * p + 1) * ng : (2 * p + 2) * ng]
                    keep = lower[:ng]
                    low.append(jnp.where(keep, one, pltpu.roll(two, KZB, 1)))
                    high.append(jnp.where(keep, pltpu.roll(one, KZB, 1), two))
                packed = jnp.concatenate(
                    [jnp.concatenate(low, axis=1), jnp.concatenate(high, axis=1)], axis=0
                )
                mixed_rows[pl.ds(at, 2 * ng), :] = packed.astype(BF)
        send_b[j] = dot(synz[...], mixed_rows[...], 1, 1).astype(BF)
        pltpu.make_async_copy(
            send_b.at[j, pl.ds(pl.multiple_of(r * zb, zb), zb)], recv_b.at[j, r], rb_sem.at[j]
        ).start()

        @pl.loop(1, nr)
        def _(t):
            to = (r + t) % nr
            pltpu.make_async_remote_copy(
                src_ref=send_b.at[j, pl.ds(pl.multiple_of(to * zb, zb), zb)],
                dst_ref=recv_b.at[j, r],
                send_sem=sb_sem.at[j], recv_sem=rb_sem.at[j],
                device_id=peer(to), device_id_type=pl.DeviceIdType.MESH,
            ).start()

    half = lax.broadcasted_iota(jnp.int32, (zb, 2 * kxl), 1) < kxl
    nxp = synx0.shape[1]
    step = min(256, nxp)

    def middle(j):
        pltpu.make_async_copy(recv_b.at[j], recv_b.at[j], rb_sem.at[j]).wait()
        for b in range(3):
            at = slice(2 * b * kxl, 2 * (b + 1) * kxl)
            for p in range(nr // 2):
                one, two = recv_b[j, 2 * p, :, at], recv_b[j, 2 * p + 1, :, at]
                to = slice(2 * p * kxl, 2 * (p + 1) * kxl)
                lhs[2 * b, :, to] = jnp.where(half, one, two)
                lhs[2 * b + 1, :, to] = jnp.where(half, two, one)
        if j == 0:
            for copy in tabs[2:6]:
                copy.wait()
        for n in range(0, nxp, step):
            cut = slice(n, n + step)
            grid = [
                dot(lhs[f], (synx0 if f % 2 == 0 else synx1)[:, cut], 1, 0) for f in range(6)
            ]
            flux[0, :, cut] = (grid[0] * grid[4] - grid[2] * grid[3]).astype(BF)
            flux[1, :, cut] = (grid[1] * grid[4] - grid[2] * grid[5]).astype(BF)
        for p in range(nr // 2):
            cut = slice(2 * p * kxl, 2 * (p + 1) * kxl)
            stream_part = dot(flux[0], slopex[:, cut], 1, 0)
            span_part = dot(flux[1], anax[:, cut], 1, 0)
            send_c[j, 2 * p] = jnp.where(half, stream_part, span_part).astype(BF)
            send_c[j, 2 * p + 1] = jnp.where(half, span_part, stream_part).astype(BF)
        pltpu.make_async_copy(send_c.at[j, r], recv_c.at[j, r], rc_sem.at[j]).start()

        @pl.loop(1, nr)
        def _(t):
            to = (r + t) % nr
            pltpu.make_async_remote_copy(
                src_ref=send_c.at[j, to], dst_ref=recv_c.at[j, r],
                send_sem=sc_sem.at[j], recv_sem=rc_sem.at[j],
                device_id=peer(to), device_id_type=pl.DeviceIdType.MESH,
            ).start()

    def backward(j):
        pltpu.make_async_copy(recv_c.at[j], recv_c.at[j], rc_sem.at[j]).wait()
        if j == 0:
            for copy in tabs[6:8]:
                copy.wait()
        parts = recv_c[j].reshape(nr * zb, 2 * kxl)
        one = dot(parts, anaz[...], 0, 0)
        two = dot(parts, slopez[...], 0, 0)
        nonlinear = -jnp.where(par == 0, one[:kxl] + two[kxl:], one[kxl:] + two[:kxl])
        keep = lower[:ng]
        for c in range(QUADS):
            for p in range(npz // 2):
                cut = slice(128 * p, 128 * p + 128)
                low = nonlinear[2 * c * ng : (2 * c + 1) * ng, cut]
                high = nonlinear[(2 * c + 1) * ng : (2 * c + 2) * ng, cut]
                back[pl.ds(2 * p * ng * QUADS + c, ng, stride=QUADS), :] = jnp.where(
                    keep, low, pltpu.roll(high, KZB, 1)
                )
                back[pl.ds((2 * p + 1) * ng * QUADS + c, ng, stride=QUADS), :] = jnp.where(
                    keep, pltpu.roll(low, KZB, 1), high
                )
        send_d[j] = back[...].astype(BF).reshape(owners, QUADS, 128)
        pltpu.make_async_copy(send_d.at[j, me], recv_d.at[j, me], rd_sem.at[j]).start()

        @pl.loop(1, owners)
        def _(t):
            to = (me + t) % owners
            pltpu.make_async_remote_copy(
                src_ref=send_d.at[j, to], dst_ref=recv_d.at[j, me],
                send_sem=sd_sem.at[j], recv_sem=rd_sem.at[j],
                device_id=owner(to), device_id_type=pl.DeviceIdType.MESH,
            ).start()

    forward(0)
    middle(0)
    forward(1)
    backward(0)
    middle(1)
    forward(2)
    backward(1)
    middle(2)
    backward(2)

    lane1 = lax.broadcasted_iota(jnp.int32, (1, 128), 1)
    kz1 = SPAN_SCALE * ((KZB // 2) * pz + (lane1 % KZB) // 2).astype(F32)
    kz_square = kz1 * kz1
    for j in range(WALLS):
        pltpu.make_async_copy(recv_d.at[j], recv_d.at[j], rd_sem.at[j]).wait()
    returned = recv_d[...].reshape(points * QUADS, 128)
    flux_coef = dot(spread[...], returned, 1, 0)
    decay = decay_ref[...]
    pieces = []
    for c in range(QUADS):
        kx1 = STREAM_SCALE * ((KXB // 2) * px + c).astype(F32)
        rates = decay + visc_ref[0] * (kz_square + kx1 * kx1)
        denom = 1.0 + IMPLICIT * rates
        old_coef = old[:, 128 * c : 128 * c + 128]
        new_coef = flux_coef[c * points : (c + 1) * points]
        mixed = (1.0 - EXPLICIT * rates) / denom * old_coef + FORCING * dt_ref[0] / denom * new_coef
        pieces.append(dot(basis_ref[...], mixed.astype(BF), 1, 0).astype(BF))
    result = dot(move[...], jnp.concatenate(pieces, axis=1), 1, 1)
    out_ref[...] = result.reshape(KZB, KXB, points).astype(BF)

    for j in range(WALLS):
        pltpu.make_async_copy(
            send_a.at[j, pl.ds(0, owners - 1)], send_a.at[j, pl.ds(0, owners - 1)], sa_sem.at[j]
        ).wait()
        pltpu.make_async_copy(
            recv_b.at[j, pl.ds(0, nr - 1)], recv_b.at[j, pl.ds(0, nr - 1)], sb_sem.at[j]
        ).wait()
        pltpu.make_async_copy(
            send_c.at[j, pl.ds(0, nr - 1)], send_c.at[j, pl.ds(0, nr - 1)], sc_sem.at[j]
        ).wait()
        pltpu.make_async_copy(
            send_d.at[j, pl.ds(0, owners - 1)], send_d.at[j, pl.ds(0, owners - 1)], sd_sem.at[j]
        ).wait()


def per_device(
    ng, nr, npz, tables,
    wall_vel, wall_slope, wall_curvature, vorticity, vort_slope,
    mean_profile, eigen_basis, eigen_decay, viscous_step, time_step,
):
    owners = ng * npz
    kxl = KXB * ng
    nkx, nkz = kxl * nr, KZB * npz
    nxp, nzp = nkx * 3 // 2, nkz * 3 // 2
    zb = nzp // nr
    points = WALLS * owners
    lanes = KZB * KXB
    hbm = pl.BlockSpec(memory_space=pl.ANY)
    vmem = pl.BlockSpec(memory_space=pltpu.VMEM)
    smem = pl.BlockSpec(memory_space=pltpu.SMEM)
    dma = pltpu.SemaphoreType.DMA
    scratch = [
        pltpu.VMEM((FIELDS, KZB, KXB, points), BF),
        *[pltpu.VMEM(t.shape, BF) for t in tables],
        pltpu.VMEM((WALLS * owners * FIELDS * QUADS, 128), F32),
        pltpu.VMEM((WALLS, owners, FIELDS, QUADS, 128), BF),
        pltpu.VMEM((WALLS, owners, FIELDS, QUADS, 128), BF),
        pltpu.VMEM((owners * FIELDS * QUADS, 128), F32),
        pltpu.VMEM((QUADS, 4, owners, 128), F32),
        pltpu.VMEM((6 * kxl, nkz), BF),
        pltpu.VMEM((WALLS, nzp, 6 * kxl), BF),
        pltpu.VMEM((WALLS, nr, zb, 6 * kxl), BF),
        pltpu.VMEM((6, zb, nkx), BF),
        pltpu.VMEM((2, zb, nxp), BF),
        pltpu.VMEM((WALLS, nr, zb, 2 * kxl), BF),
        pltpu.VMEM((WALLS, nr, zb, 2 * kxl), BF),
        pltpu.VMEM((owners * QUADS, 128), F32),
        pltpu.VMEM((WALLS, owners, QUADS, 128), BF),
        pltpu.VMEM((WALLS, owners, QUADS, 128), BF),
        pltpu.VMEM((points, lanes), F32),
        pltpu.VMEM((points * QUADS, points * QUADS), BF),
        dma((FIELDS,)),
        dma((len(tables),)),
        dma((1,)),
        *[dma((WALLS,)) for _ in range(8)],
    ]
    return pl.pallas_call(
        functools.partial(kernel_body, ng, nr, npz),
        out_shape=jax.ShapeDtypeStruct(vorticity.shape, BF),
        in_specs=[hbm] * (FIELDS + len(tables)) + [smem, vmem, vmem, smem, smem],
        out_specs=vmem,
        scratch_shapes=scratch,
        compiler_params=pltpu.CompilerParams(
            collective_id=0, has_side_effects=True, vmem_limit_bytes=56 * 1024 * 1024
        ),
    )(
        wall_slope, wall_curvature, vorticity, vort_slope, wall_vel,
        *[jnp.asarray(t) for t in tables],
        mean_profile, eigen_basis, eigen_decay[:, None], viscous_step, time_step,
    )


def build(mesh, nr):
    npz = mesh.shape["pz"]
    ng = mesh.shape["px"] // nr
    tables = all_tables(ng, nr, npz)
    spec = P("pz", "px", None)
    return jax.shard_map(
        functools.partial(per_device, ng, nr, npz, tables),
        mesh=mesh,
        in_specs=(spec,) * 5 + (P(),) * 5,
        out_specs=spec,
        check_vma=False,
    )


def solution(mesh):
    return build(mesh, NR)
```

```python
import functools
import math

import jax
import jax.numpy as jnp
import ml_dtypes
import numpy as np
from jax import lax
from jax.experimental import pallas as pl
from jax.experimental.pallas import tpu as pltpu
from jax.sharding import PartitionSpec as P

NR = 8
WALLS = 3
FIELDS = 5
QUADS = 4
KZB = 64
KXB = 8

STREAM_SCALE = 0.25
SPAN_SCALE = 2.0 / 3.0
EXPLICIT = 29.0 / 96.0
IMPLICIT = 37.0 / 160.0
FORCING = 8.0 / 15.0

BF = jnp.bfloat16
F32 = jnp.float32

SLOPE, VORT, VEL, CURV, VSLOPE = range(FIELDS)
EARLY = 3


def make_tables(count, points, scale):
    indices = np.arange(count)
    number = indices // 2
    cosine = (indices % 2 == 0)[:, None]
    phase = number[:, None] * np.arange(points)[None, :] % points
    angles = phase * (2.0 * math.pi / points)
    cos_part, sin_part = np.cos(angles), np.sin(angles)
    shape_rows = np.where(cosine, cos_part, sin_part)
    norm = math.sqrt(2.0 / count)
    synthesis = norm * shape_rows
    analysis = (2.0 / points / norm * shape_rows).T
    slope_rows = np.where(cosine, sin_part, -cos_part)
    slope_analysis = ((scale * number)[:, None] * (2.0 / points / norm) * slope_rows).T

    def rounded(t):
        return t.astype(np.float32).astype(ml_dtypes.bfloat16)

    return rounded(synthesis), rounded(analysis), rounded(slope_analysis)


def all_tables(ng, nr, npz):
    kxb = KXB * ng
    nkx, nkz = kxb * nr, KZB * npz
    syn_x, ana_x, slope_x = make_tables(nkx, nkx * 3 // 2, STREAM_SCALE)
    syn_z, ana_z, slope_z = make_tables(nkz, nkz * 3 // 2, SPAN_SCALE)
    r, c, m, g = np.meshgrid(
        np.arange(nr), np.arange(QUADS), np.arange(2), np.arange(ng), indexing="ij"
    )
    order = (g * (KXB * nr) + r * KXB + 2 * c + m).reshape(nr, kxb)
    plain = order.reshape(-1)
    crossed = order.reshape(nr // 2, 2, kxb)[:, ::-1].reshape(-1)
    rows = KZB * KXB
    move = np.zeros((rows, rows), np.float32)
    kz, kx = np.meshgrid(np.arange(KZB), np.arange(KXB), indexing="ij")
    move[(kz * KXB + kx).reshape(-1), (kx * KZB + kz).reshape(-1)] = 1.0
    return (
        move.astype(ml_dtypes.bfloat16),
        np.ascontiguousarray(syn_z.T),
        np.ascontiguousarray(syn_x[plain]),
        np.ascontiguousarray(syn_x[crossed]),
        np.ascontiguousarray(slope_x[:, plain]),
        np.ascontiguousarray(ana_x[:, crossed]),
        ana_z,
        slope_z,
    )


def dot(a, b, ca, cb):
    return lax.dot_general(a, b, (((ca,), (cb,)), ((), ())), preferred_element_type=F32)


def kernel_body(
    ng, nr, npz,
    slope_h, vort_h, vel_h, curv_h, vslope_h,
    move_h, synz_h, synx0_h, synx1_h, slopex_h, anax_h, anaz_h, slopez_h,
    basis_h, decay_h, mean_ref, visc_ref, dt_ref,
    out_ref,
    xin, move, synz, synx0, synx1, slopex, anax, anaz, slopez, basis_ref, decay_ref,
    stage, send_a, recv_a, wide, coef, mixed_rows, send_b, recv_b, lhs, grids, flux,
    send_c, recv_c, back, send_d, recv_d, old, spread,
    in_sem, tab_sem, sa_sem, ra_sem, sb_sem, rb_sem, sc_sem, rc_sem, sd_sem, rd_sem,
):
    owners = ng * npz
    kxl = KXB * ng
    zb = synz.shape[0] // nr
    nxp = synx0.shape[1]
    points = WALLS * owners
    px = lax.axis_index("px")
    pz = lax.axis_index("pz")
    g = px // nr
    r = px % nr
    me = pz * ng + g
    par = r % 2
    ny, nz = ng // 2, 2 * npz
    y = g // 2
    z = (g % 2) * npz + pz

    def each_owner(act):
        def at(dz, dy):
            z2 = (z + dz) % nz
            g2 = (y + dy) % ny * 2 + z2 // npz
            p2 = z2 % npz
            act(p2 * ng + g2, {"px": g2 * nr + r, "pz": p2})

        @pl.loop(0, nz - 1)
        def _(k):
            up, down = nz // 2 + (k + 1) // 2, nz // 2 - k // 2
            dz = k % 2 * up + (1 - k % 2) * down
            for dy in range(ny):
                at(dz, dy)

        for dy in range(1, ny):
            at(0, dy)

    def each_peer(act):
        @pl.loop(1, nr)
        def _(t):
            q = (r + t) % nr
            act(q, {"px": g * nr + q, "pz": pz})

    def remote(src, dst, send_sem, recv_sem, device):
        pltpu.make_async_remote_copy(
            src_ref=src, dst_ref=dst, send_sem=send_sem, recv_sem=recv_sem,
            device_id=device, device_id_type=pl.DeviceIdType.MESH,
        ).start()

    def await_all(ref, sem):
        pltpu.make_async_copy(ref, ref, sem).wait()

    barrier = pltpu.get_barrier_semaphore()

    def greet(_, device):
        pl.semaphore_signal(
            barrier, inc=1, device_id=device, device_id_type=pl.DeviceIdType.MESH
        )

    each_owner(greet)
    each_peer(greet)

    tabs = [
        pltpu.make_async_copy(h, v, tab_sem.at[i])
        for i, (h, v) in enumerate(
            (
                (move_h, move), (synz_h, synz), (synx0_h, synx0), (synx1_h, synx1),
                (slopex_h, slopex), (anax_h, anax), (anaz_h, anaz), (slopez_h, slopez),
                (basis_h, basis_ref), (decay_h, decay_ref),
            )
        )
    ]
    ins = [
        pltpu.make_async_copy(h, xin.at[i], in_sem.at[i])
        for i, h in enumerate((slope_h, vort_h, vel_h, curv_h, vslope_h))
    ]
    tabs[0].start()
    for copy in ins:
        copy.start()
    for copy in tabs[8:] + tabs[1:8]:
        copy.start()

    tabs[0].wait()
    per_owner = FIELDS * QUADS
    for i in range(FIELDS):
        ins[i].wait()
        block = xin[i].reshape(KZB * KXB, points)
        turned = dot(block, move[...], 0, 0)
        for j in range(WALLS):
            for c in range(QUADS):
                stage[pl.ds(j * owners * per_owner + i * QUADS + c, owners, stride=per_owner), :] = (
                    turned[j * owners : (j + 1) * owners, 128 * c : 128 * c + 128]
                )
        if i == VORT:
            old[...] = turned

    pieces = [(j, 0, FIELDS) for j in range(WALLS - 1)]
    pieces += [(WALLS - 1, 0, EARLY), (WALLS - 1, EARLY, FIELDS)]
    for n, (j, lo, hi) in enumerate(pieces):
        if lo == 0:
            rows = owners * per_owner
            send_a[j] = (
                stage[j * rows : (j + 1) * rows, :].astype(BF).reshape(owners, FIELDS, QUADS, 128)
            )
        if n == 0:
            pl.semaphore_wait(barrier, owners - 1 + nr - 1)
        pltpu.make_async_copy(
            send_a.at[j, me, pl.ds(lo, hi - lo)], recv_a.at[j, me, pl.ds(lo, hi - lo)], ra_sem.at[n]
        ).start()

        def send(to, device, n=n, j=j, part=pl.ds(lo, hi - lo)):
            remote(
                send_a.at[j, to, part], recv_a.at[j, me, part], sa_sem.at[n], ra_sem.at[n], device
            )

        each_owner(send)

    row = lax.broadcasted_iota(jnp.int32, (owners, 128), 0)
    lane = lax.broadcasted_iota(jnp.int32, (owners, 128), 1)
    lower = lane < KZB
    even = lane % 2 == 0
    kz_rate = SPAN_SCALE * ((KZB // 2) * (row // ng) + (lane % KZB) // 2).astype(F32)
    fz = jnp.where(even, kz_rate, -kz_rate)
    for c in range(QUADS):
        number = (KXB // 2) * nr * (row % ng) + (KXB // 2) * r + c
        kx_rate = STREAM_SCALE * number.astype(F32)
        fx = jnp.where(lower, kx_rate, -kx_rate)
        square = kx_rate * kx_rate + kz_rate * kz_rate
        safe = jnp.where(square == 0.0, 1.0, square)
        coef[c, 0] = fx
        coef[c, 1] = fx / safe
        coef[c, 2] = fz / safe
    coef[0, 3] = fz

    tabs[8].wait()
    tabs[9].wait()
    col = lax.broadcasted_iota(jnp.int32, (points, points * QUADS), 1)
    point = lax.broadcasted_iota(jnp.int32, (points, points * QUADS), 0)
    wide_basis = dot(
        basis_ref[...], jnp.where(col // QUADS == point, 1.0, 0.0).astype(BF), 0, 0
    )
    for c in range(QUADS):
        spread[c * points : (c + 1) * points, :] = jnp.where(
            col % QUADS == c, wide_basis, 0.0
        ).astype(BF)
    old[...] = dot(basis_ref[...], old[...].astype(BF), 0, 0)

    def swap_x(v):
        return pltpu.roll(v, KZB, 1)

    def swap_z(v):
        return jnp.where(even, pltpu.roll(v, 127, 1), pltpu.roll(v, 1, 1))

    first = (row == 0) & (lane == 0) & (r == 0)

    def unpack(j, lo, hi):
        rows = (hi - lo) * QUADS
        wide[0 : owners * rows, :] = (
            recv_a[j, :, lo:hi].reshape(owners * rows, 128).astype(F32)
        )
        return lambda i, c: wide[pl.ds((i - lo) * QUADS + c, owners, stride=rows), :]

    def place(f, c, field):
        at = pl.multiple_of((f + par - 2 * par * (f % 2)) * kxl + c * 2 * ng, 2 * ng)
        keep = lower[:ng]
        low, high = [], []
        for p in range(npz // 2):
            one = field[2 * p * ng : (2 * p + 1) * ng]
            two = field[(2 * p + 1) * ng : (2 * p + 2) * ng]
            low.append(jnp.where(keep, one, pltpu.roll(two, KZB, 1)))
            high.append(jnp.where(keep, pltpu.roll(one, KZB, 1), two))
        packed = jnp.concatenate(
            [jnp.concatenate(low, axis=1), jnp.concatenate(high, axis=1)], axis=0
        )
        mixed_rows[pl.ds(at, 2 * ng), :] = packed.astype(BF)

    def exchange_b(j, lo, hi):
        width = 2 * kxl
        made = dot(synz[...], mixed_rows[lo * width : hi * width, :], 1, 1).astype(BF)
        for b in range(lo, hi):
            send_b[j, b] = made[:, (b - lo) * width : (b - lo + 1) * width]
        part = pl.ds(lo, hi - lo)
        n = 2 * j + (lo > 0)

        def rows(q):
            return send_b.at[j, part, pl.ds(pl.multiple_of(q * zb, zb), zb)]

        pltpu.make_async_copy(rows(r), recv_b.at[j, r, part], rb_sem.at[n]).start()
        each_peer(
            lambda q, device: remote(
                rows(q), recv_b.at[j, r, part], sb_sem.at[n], rb_sem.at[n], device
            )
        )

    def mean(i, j):
        return jnp.where(first, mean_ref[i, owners * j + me], 0.0)

    def forward_early(j):
        load = unpack(j, 0, EARLY)
        for c in range(QUADS):
            s, o, v = load(SLOPE, c), load(VORT, c), load(VEL, c)
            a, b = coef[c, 1], coef[c, 2]
            stream_vel = swap_z(b * o) - swap_x(a * s)
            span_vel = -swap_z(b * s) - swap_x(a * o)
            if c == 0:
                stream_vel += mean(0, j)
                span_vel += mean(1, j)
            for f, field in enumerate((stream_vel, span_vel, v, o)):
                place(f, c, field)
        exchange_b(j, 0, 2)

    def forward_late(j):
        load = unpack(j, VEL, FIELDS)
        for c in range(QUADS):
            v, cv, q = load(VEL, c), load(CURV, c), load(VSLOPE, c)
            fx, a, b, fzz = coef[c, 0], coef[c, 1], coef[c, 2], coef[0, 3]
            stream_vort = swap_z(fzz * v - b * cv) - swap_x(a * q)
            span_vort = swap_x(a * cv - fx * v) - swap_z(b * q)
            if c == 0:
                stream_vort += mean(3, j)
                span_vort -= mean(2, j)
            place(4, c, stream_vort)
            place(5, c, span_vort)
        exchange_b(j, 2, 3)

    half = lax.broadcasted_iota(jnp.int32, (zb, 2 * kxl), 1) < kxl

    def gather_b(j, lo, hi):
        await_all(recv_b.at[j, :, pl.ds(lo, hi - lo)], rb_sem.at[2 * j + (lo > 0)])
        for b in range(lo, hi):
            for p in range(nr // 2):
                one, two = recv_b[j, 2 * p, b], recv_b[j, 2 * p + 1, b]
                to = slice(2 * p * kxl, 2 * (p + 1) * kxl)
                lhs[2 * b, :, to] = jnp.where(half, one, two)
                lhs[2 * b + 1, :, to] = jnp.where(half, two, one)

    def grid(f, cut):
        return dot(lhs[f], (synx0 if f % 2 == 0 else synx1)[:, cut], 1, 0)

    cuts = [slice(n, n + min(256, nxp)) for n in range(0, nxp, min(256, nxp))]

    def middle_early(j):
        gather_b(j, 0, 2)
        for cut in cuts:
            for f in range(4):
                grids[f, :, cut] = grid(f, cut)

    def middle_late(j):
        gather_b(j, 2, 3)
        for cut in cuts:
            v, o = grids[2, :, cut], grids[3, :, cut]
            flux[0, :, cut] = (grids[0, :, cut] * o - v * grid(4, cut)).astype(BF)
            flux[1, :, cut] = (grids[1, :, cut] * o - v * grid(5, cut)).astype(BF)
        for p in range(nr // 2):
            cut = slice(2 * p * kxl, 2 * (p + 1) * kxl)
            stream_part = dot(flux[0], slopex[:, cut], 1, 0)
            span_part = dot(flux[1], anax[:, cut], 1, 0)
            send_c[j, 2 * p] = jnp.where(half, stream_part, span_part).astype(BF)
            send_c[j, 2 * p + 1] = jnp.where(half, span_part, stream_part).astype(BF)
        pltpu.make_async_copy(send_c.at[j, r], recv_c.at[j, r], rc_sem.at[j]).start()
        each_peer(
            lambda q, device: remote(
                send_c.at[j, q], recv_c.at[j, r], sc_sem.at[j], rc_sem.at[j], device
            )
        )

    def backward(j):
        await_all(recv_c.at[j], rc_sem.at[j])
        parts = recv_c[j].reshape(nr * zb, 2 * kxl)
        one = dot(parts, anaz[...], 0, 0)
        two = dot(parts, slopez[...], 0, 0)
        nonlinear = -jnp.where(par == 0, one[:kxl] + two[kxl:], one[kxl:] + two[:kxl])
        keep = lower[:ng]
        for c in range(QUADS):
            for p in range(npz // 2):
                cut = slice(128 * p, 128 * p + 128)
                low = nonlinear[2 * c * ng : (2 * c + 1) * ng, cut]
                high = nonlinear[(2 * c + 1) * ng : (2 * c + 2) * ng, cut]
                back[pl.ds(2 * p * ng * QUADS + c, ng, stride=QUADS), :] = jnp.where(
                    keep, low, pltpu.roll(high, KZB, 1)
                )
                back[pl.ds((2 * p + 1) * ng * QUADS + c, ng, stride=QUADS), :] = jnp.where(
                    keep, pltpu.roll(low, KZB, 1), high
                )
        send_d[j] = back[...].astype(BF).reshape(owners, QUADS, 128)

    def exchange_d(j):
        pltpu.make_async_copy(send_d.at[j, me], recv_d.at[j, me], rd_sem.at[j]).start()
        each_owner(
            lambda to, device: remote(
                send_d.at[j, to], recv_d.at[j, me], sd_sem.at[j], rd_sem.at[j], device
            )
        )

    await_all(recv_a.at[0], ra_sem.at[0])
    tabs[1].wait()
    forward_early(0)
    forward_late(0)
    tabs[2].wait()
    tabs[3].wait()
    middle_early(0)
    tabs[4].wait()
    tabs[5].wait()
    middle_late(0)
    await_all(recv_a.at[1], ra_sem.at[1])
    forward_early(1)
    forward_late(1)
    tabs[6].wait()
    tabs[7].wait()
    backward(0)
    middle_early(1)
    middle_late(1)
    await_all(recv_a.at[2, :, pl.ds(0, EARLY)], ra_sem.at[2])
    forward_early(2)
    backward(1)
    await_all(recv_a.at[2, :, pl.ds(EARLY, FIELDS - EARLY)], ra_sem.at[3])
    forward_late(2)
    exchange_d(0)
    middle_early(2)
    middle_late(2)
    exchange_d(1)
    backward(2)
    exchange_d(2)

    decay = jnp.transpose(jnp.broadcast_to(decay_ref[...], (128, points)))
    lane1 = lax.broadcasted_iota(jnp.int32, (1, 128), 1)
    kz1 = SPAN_SCALE * ((KZB // 2) * pz + (lane1 % KZB) // 2).astype(F32)
    kz_square = kz1 * kz1
    for j in range(WALLS):
        await_all(recv_d.at[j], rd_sem.at[j])
    flux_coef = dot(spread[...], recv_d[...].reshape(points * QUADS, 128), 1, 0)
    solved = []
    for c in range(QUADS):
        kx1 = STREAM_SCALE * ((KXB // 2) * px + c).astype(F32)
        rates = decay + visc_ref[0] * (kz_square + kx1 * kx1)
        denom = 1.0 + IMPLICIT * rates
        old_coef = old[:, 128 * c : 128 * c + 128]
        new_coef = flux_coef[c * points : (c + 1) * points]
        mixed = (1.0 - EXPLICIT * rates) / denom * old_coef + FORCING * dt_ref[0] / denom * new_coef
        solved.append(dot(basis_ref[...], mixed.astype(BF), 1, 0).astype(BF))
    result = dot(move[...], jnp.concatenate(solved, axis=1), 1, 1)
    out_ref[...] = result.astype(BF).reshape(out_ref.shape)

    for n, (j, lo, hi) in enumerate(pieces):
        await_all(send_a.at[j, pl.ds(0, owners - 1), pl.ds(lo, hi - lo)], sa_sem.at[n])
    for j in range(WALLS):
        await_all(recv_b.at[j, pl.ds(0, nr - 1), pl.ds(0, 2)], sb_sem.at[2 * j])
        await_all(recv_b.at[j, pl.ds(0, nr - 1), pl.ds(2, 1)], sb_sem.at[2 * j + 1])
        await_all(send_c.at[j, pl.ds(0, nr - 1)], sc_sem.at[j])
        await_all(send_d.at[j, pl.ds(0, owners - 1)], sd_sem.at[j])


def per_device(
    ng, nr, npz, tables,
    wall_vel, wall_slope, wall_curvature, vorticity, vort_slope,
    mean_profile, eigen_basis, eigen_decay, viscous_step, time_step,
):
    owners = ng * npz
    kxl = KXB * ng
    nkx, nkz = kxl * nr, KZB * npz
    nxp, nzp = nkx * 3 // 2, nkz * 3 // 2
    zb = nzp // nr
    points = WALLS * owners
    lanes = KZB * KXB
    hbm = pl.BlockSpec(memory_space=pl.ANY)
    vmem = pl.BlockSpec(memory_space=pltpu.VMEM)
    smem = pl.BlockSpec(memory_space=pltpu.SMEM)
    dma = pltpu.SemaphoreType.DMA
    scratch = [
        pltpu.VMEM((FIELDS, KZB, KXB, points), BF),
        *[pltpu.VMEM(t.shape, BF) for t in tables],
        pltpu.VMEM((points, points), BF),
        pltpu.VMEM((1, points), F32),
        pltpu.VMEM((WALLS * owners * FIELDS * QUADS, 128), F32),
        pltpu.VMEM((WALLS, owners, FIELDS, QUADS, 128), BF),
        pltpu.VMEM((WALLS, owners, FIELDS, QUADS, 128), BF),
        pltpu.VMEM((owners * EARLY * QUADS, 128), F32),
        pltpu.VMEM((QUADS, 4, owners, 128), F32),
        pltpu.VMEM((6 * kxl, nkz), BF),
        pltpu.VMEM((WALLS, 3, nzp, 2 * kxl), BF),
        pltpu.VMEM((WALLS, nr, 3, zb, 2 * kxl), BF),
        pltpu.VMEM((6, zb, nkx), BF),
        pltpu.VMEM((4, zb, nxp), F32),
        pltpu.VMEM((2, zb, nxp), BF),
        pltpu.VMEM((WALLS, nr, zb, 2 * kxl), BF),
        pltpu.VMEM((WALLS, nr, zb, 2 * kxl), BF),
        pltpu.VMEM((owners * QUADS, 128), F32),
        pltpu.VMEM((WALLS, owners, QUADS, 128), BF),
        pltpu.VMEM((WALLS, owners, QUADS, 128), BF),
        pltpu.VMEM((points, lanes), F32),
        pltpu.VMEM((points * QUADS, points * QUADS), BF),
        dma((FIELDS,)),
        dma((len(tables) + 2,)),
        *[dma((WALLS + 1,)) for _ in range(2)],
        *[dma((2 * WALLS,)) for _ in range(2)],
        *[dma((WALLS,)) for _ in range(4)],
    ]
    out = pl.pallas_call(
        functools.partial(kernel_body, ng, nr, npz),
        out_shape=jax.ShapeDtypeStruct((lanes, points), BF),
        in_specs=[hbm] * (FIELDS + len(tables) + 2) + [smem] * 3,
        out_specs=vmem,
        scratch_shapes=scratch,
        compiler_params=pltpu.CompilerParams(
            collective_id=0, has_side_effects=True, vmem_limit_bytes=60 * 1024 * 1024
        ),
    )(
        wall_slope, vorticity, wall_vel, wall_curvature, vort_slope,
        *[jnp.asarray(t) for t in tables],
        eigen_basis, eigen_decay.reshape(1, points), mean_profile, viscous_step, time_step,
    )
    return out.reshape(vorticity.shape)


def build(mesh, nr):
    npz = mesh.shape["pz"]
    ng = mesh.shape["px"] // nr
    tables = all_tables(ng, nr, npz)
    spec = P("pz", "px", None)
    return jax.shard_map(
        functools.partial(per_device, ng, nr, npz, tables),
        mesh=mesh,
        in_specs=(spec,) * 5 + (P(),) * 5,
        out_specs=spec,
        check_vma=False,
    )


def solution(mesh):
    return build(mesh, NR)
```

```python
import functools
import math

import jax
import jax.numpy as jnp
import ml_dtypes
import numpy as np
from jax import lax
from jax.experimental import pallas as pl
from jax.experimental.pallas import tpu as pltpu
from jax.sharding import PartitionSpec as P

NR = 8
WALLS = 3
FIELDS = 5
QUADS = 4
KZB = 64
KXB = 8

STREAM_SCALE = 0.25
SPAN_SCALE = 2.0 / 3.0
EXPLICIT = 29.0 / 96.0
IMPLICIT = 37.0 / 160.0
FORCING = 8.0 / 15.0

BF = jnp.bfloat16
F32 = jnp.float32

SLOPE, VORT, VEL, CURV, VSLOPE = range(FIELDS)
EARLY = 3


def make_tables(count, points, scale):
    indices = np.arange(count)
    number = indices // 2
    cosine = (indices % 2 == 0)[:, None]
    phase = number[:, None] * np.arange(points)[None, :] % points
    angles = phase * (2.0 * math.pi / points)
    cos_part, sin_part = np.cos(angles), np.sin(angles)
    shape_rows = np.where(cosine, cos_part, sin_part)
    norm = math.sqrt(2.0 / count)
    synthesis = norm * shape_rows
    analysis = (2.0 / points / norm * shape_rows).T
    slope_rows = np.where(cosine, sin_part, -cos_part)
    slope_analysis = ((scale * number)[:, None] * (2.0 / points / norm) * slope_rows).T

    def rounded(t):
        return t.astype(np.float32).astype(ml_dtypes.bfloat16)

    return rounded(synthesis), rounded(analysis), rounded(slope_analysis)


def all_tables(ng, nr, npz):
    kxb = KXB * ng
    nkx, nkz = kxb * nr, KZB * npz
    syn_x, ana_x, slope_x = make_tables(nkx, nkx * 3 // 2, STREAM_SCALE)
    syn_z, ana_z, slope_z = make_tables(nkz, nkz * 3 // 2, SPAN_SCALE)
    r, c, m, g = np.meshgrid(
        np.arange(nr), np.arange(QUADS), np.arange(2), np.arange(ng), indexing="ij"
    )
    order = (g * (KXB * nr) + r * KXB + 2 * c + m).reshape(nr, kxb)
    plain = order.reshape(-1)
    crossed = order.reshape(nr // 2, 2, kxb)[:, ::-1].reshape(-1)
    rows = KZB * KXB
    move = np.zeros((rows, rows), np.float32)
    kz, kx = np.meshgrid(np.arange(KZB), np.arange(KXB), indexing="ij")
    move[(kz * KXB + kx).reshape(-1), (kx * KZB + kz).reshape(-1)] = 1.0
    return (
        move.astype(ml_dtypes.bfloat16),
        np.ascontiguousarray(syn_z.T),
        np.ascontiguousarray(syn_x[plain]),
        np.ascontiguousarray(syn_x[crossed]),
        np.ascontiguousarray(slope_x[:, plain]),
        np.ascontiguousarray(ana_x[:, crossed]),
        ana_z,
        slope_z,
    )


def dot(a, b, ca, cb):
    return lax.dot_general(a, b, (((ca,), (cb,)), ((), ())), preferred_element_type=F32)


def kernel_body(
    ng, nr, npz,
    slope_h, vort_h, vel_h, curv_h, vslope_h,
    move_h, synz_h, synx0_h, synx1_h, slopex_h, anax_h, anaz_h, slopez_h,
    basis_h, decay_h, mean_h, visc_h, dt_h,
    out_ref,
    xin, move, synz, synx0, synx1, slopex, anax, anaz, slopez, basis_ref, decay_ref,
    mean_ref, visc_ref, dt_ref,
    stage, send_a, recv_a, wide, coef, mixed_rows, send_b, recv_b, lhs, grids, flux,
    send_c, recv_c, back, send_d, recv_d, old, gain, flux_coef, spread,
    in_sem, tab_sem, sa_sem, ra_sem, sb_sem, rb_sem, sc_sem, rc_sem, sd_sem, rd_sem,
):
    owners = ng * npz
    kxl = KXB * ng
    zb = synz.shape[0] // nr
    nxp = synx0.shape[1]
    points = WALLS * owners
    px = lax.axis_index("px")
    pz = lax.axis_index("pz")
    g = px // nr
    r = px % nr
    me = pz * ng + g
    par = r % 2
    ny, nz = ng // 2, 2 * npz
    y = g // 2
    z = (g % 2) * npz + pz

    def each_owner(act):
        far_first = sorted(range(ny), key=lambda dy: -min(dy, ny - dy))

        def at(dz, dy):
            z2 = (z + dz) % nz
            g2 = (y + dy) % ny * 2 + z2 // npz
            p2 = z2 % npz
            act(p2 * ng + g2, {"px": g2 * nr + r, "pz": p2})

        @pl.loop(0, nz - 1)
        def _(k):
            up, down = nz // 2 + (k + 1) // 2, nz // 2 - k // 2
            dz = k % 2 * up + (1 - k % 2) * down
            for dy in far_first:
                at(dz, dy)

        for dy in far_first[:-1]:
            at(0, dy)

    def each_peer(act):
        for t in sorted(range(1, nr), key=lambda t: -min(t, nr - t)):
            q = (r + t) % nr
            act(q, {"px": g * nr + q, "pz": pz})

    def remote(src, dst, send_sem, recv_sem, device):
        pltpu.make_async_remote_copy(
            src_ref=src, dst_ref=dst, send_sem=send_sem, recv_sem=recv_sem,
            device_id=device, device_id_type=pl.DeviceIdType.MESH,
        ).start()

    def local(src, dst, sem):
        pltpu.make_async_copy(src, dst, sem).start()

    def await_all(ref, sem):
        pltpu.make_async_copy(ref, ref, sem).wait()

    barrier = pltpu.get_barrier_semaphore()

    def greet(_, device):
        pl.semaphore_signal(
            barrier, inc=1, device_id=device, device_id_type=pl.DeviceIdType.MESH
        )

    each_owner(greet)
    each_peer(greet)

    tabs = [
        pltpu.make_async_copy(h, v, tab_sem.at[i])
        for i, (h, v) in enumerate(
            (
                (move_h, move), (synz_h, synz), (synx0_h, synx0), (synx1_h, synx1),
                (slopex_h, slopex), (anax_h, anax), (anaz_h, anaz), (slopez_h, slopez),
                (basis_h, basis_ref), (decay_h, decay_ref),
                (mean_h, mean_ref), (visc_h, visc_ref), (dt_h, dt_ref),
            )
        )
    ]
    ins = [
        pltpu.make_async_copy(h, xin.at[i], in_sem.at[i])
        for i, h in enumerate((slope_h, vort_h, vel_h, curv_h, vslope_h))
    ]
    tabs[0].start()
    for copy in ins:
        copy.start()
    for copy in tabs[8:] + tabs[1:8]:
        copy.start()

    tabs[0].wait()
    per_owner = FIELDS * QUADS
    for i in range(FIELDS):
        ins[i].wait()
        block = xin[i].reshape(KZB * KXB, points)
        turned = dot(block, move[...], 0, 0)
        for j in range(WALLS):
            for c in range(QUADS):
                stage[pl.ds(j * owners * per_owner + i * QUADS + c, owners, stride=per_owner), :] = (
                    turned[j * owners : (j + 1) * owners, 128 * c : 128 * c + 128]
                )
        if i == VORT:
            old[...] = turned

    pieces = [(j, 0, FIELDS) for j in range(WALLS - 1)]
    pieces += [(WALLS - 1, 0, EARLY), (WALLS - 1, EARLY, FIELDS)]
    for n, (j, lo, hi) in enumerate(pieces):
        if lo == 0:
            rows = owners * per_owner
            send_a[j] = (
                stage[j * rows : (j + 1) * rows, :].astype(BF).reshape(owners, FIELDS, QUADS, 128)
            )
        if n == 0:
            pl.semaphore_wait(barrier, owners - 1 + nr - 1)
        part = pl.ds(lo, hi - lo)
        local(send_a.at[j, me, part], recv_a.at[j, me, part], ra_sem.at[n])

        def send(to, device, n=n, j=j, part=part):
            remote(
                send_a.at[j, to, part], recv_a.at[j, me, part], sa_sem.at[n], ra_sem.at[n], device
            )

        each_owner(send)

    row = lax.broadcasted_iota(jnp.int32, (owners, 128), 0)
    lane = lax.broadcasted_iota(jnp.int32, (owners, 128), 1)
    lower = lane < KZB
    even = lane % 2 == 0
    kz_rate = SPAN_SCALE * ((KZB // 2) * (row // ng) + (lane % KZB) // 2).astype(F32)
    fz = jnp.where(even, kz_rate, -kz_rate)
    for c in range(QUADS):
        number = (KXB // 2) * nr * (row % ng) + (KXB // 2) * r + c
        kx_rate = STREAM_SCALE * number.astype(F32)
        fx = jnp.where(lower, kx_rate, -kx_rate)
        square = kx_rate * kx_rate + kz_rate * kz_rate
        safe = jnp.where(square == 0.0, 1.0, square)
        coef[c, 0] = fx
        coef[c, 1] = fx / safe
        coef[c, 2] = fz / safe
    coef[0, 3] = fz

    for copy in tabs[8:]:
        copy.wait()
    col = lax.broadcasted_iota(jnp.int32, (points, points * QUADS), 1)
    point = lax.broadcasted_iota(jnp.int32, (points, points * QUADS), 0)
    wide_basis = dot(
        basis_ref[...], jnp.where(col // QUADS == point, 1.0, 0.0).astype(BF), 0, 0
    )
    for c in range(QUADS):
        spread[c * points : (c + 1) * points, :] = jnp.where(
            col % QUADS == c, wide_basis, 0.0
        ).astype(BF)
    old[...] = dot(basis_ref[...], old[...].astype(BF), 0, 0)

    def swap_x(v):
        return pltpu.roll(v, KZB, 1)

    def swap_z(v):
        return jnp.where(even, pltpu.roll(v, 127, 1), pltpu.roll(v, 1, 1))

    first = (row == 0) & (lane == 0) & (r == 0)

    def unpack(j, lo, hi):
        rows = (hi - lo) * QUADS
        wide[0 : owners * rows, :] = (
            recv_a[j, :, lo:hi].reshape(owners * rows, 128).astype(F32)
        )
        return lambda i, c: wide[pl.ds((i - lo) * QUADS + c, owners, stride=rows), :]

    def place(f, c, field):
        at = pl.multiple_of((f + par - 2 * par * (f % 2)) * kxl + c * 2 * ng, 2 * ng)
        keep = lower[:ng]
        low, high = [], []
        for p in range(npz // 2):
            one = field[2 * p * ng : (2 * p + 1) * ng]
            two = field[(2 * p + 1) * ng : (2 * p + 2) * ng]
            low.append(jnp.where(keep, one, pltpu.roll(two, KZB, 1)))
            high.append(jnp.where(keep, pltpu.roll(one, KZB, 1), two))
        packed = jnp.concatenate(
            [jnp.concatenate(low, axis=1), jnp.concatenate(high, axis=1)], axis=0
        )
        mixed_rows[pl.ds(at, 2 * ng), :] = packed.astype(BF)

    def exchange_b(j, lo, hi):
        width = 2 * kxl
        made = dot(synz[...], mixed_rows[lo * width : hi * width, :], 1, 1).astype(BF)
        for b in range(lo, hi):
            send_b[j, b] = made[:, (b - lo) * width : (b - lo + 1) * width]
        part = pl.ds(lo, hi - lo)
        n = 2 * j + (lo > 0)

        def rows(q):
            return send_b.at[j, part, pl.ds(pl.multiple_of(q * zb, zb), zb)]

        local(rows(r), recv_b.at[j, r, part], rb_sem.at[n])
        each_peer(
            lambda q, device: remote(
                rows(q), recv_b.at[j, r, part], sb_sem.at[n], rb_sem.at[n], device
            )
        )

    def mean(i, j):
        return jnp.where(first, mean_ref[i, owners * j + me], 0.0)

    def forward_early(j):
        load = unpack(j, 0, EARLY)
        for c in range(QUADS):
            s, o, v = load(SLOPE, c), load(VORT, c), load(VEL, c)
            a, b = coef[c, 1], coef[c, 2]
            stream_vel = swap_z(b * o) - swap_x(a * s)
            span_vel = -swap_z(b * s) - swap_x(a * o)
            if c == 0:
                stream_vel += mean(0, j)
                span_vel += mean(1, j)
            for f, field in enumerate((stream_vel, span_vel, v, o)):
                place(f, c, field)
        exchange_b(j, 0, 2)

    def forward_late(j):
        load = unpack(j, VEL, FIELDS)
        for c in range(QUADS):
            v, cv, q = load(VEL, c), load(CURV, c), load(VSLOPE, c)
            fx, a, b, fzz = coef[c, 0], coef[c, 1], coef[c, 2], coef[0, 3]
            stream_vort = swap_z(fzz * v - b * cv) - swap_x(a * q)
            span_vort = swap_x(a * cv - fx * v) - swap_z(b * q)
            if c == 0:
                stream_vort += mean(3, j)
                span_vort -= mean(2, j)
            place(4, c, stream_vort)
            place(5, c, span_vort)
        exchange_b(j, 2, 3)

    half = lax.broadcasted_iota(jnp.int32, (zb, 2 * kxl), 1) < kxl

    def gather_b(j, lo, hi):
        await_all(recv_b.at[j, :, pl.ds(lo, hi - lo)], rb_sem.at[2 * j + (lo > 0)])
        for b in range(lo, hi):
            for p in range(nr // 2):
                one, two = recv_b[j, 2 * p, b], recv_b[j, 2 * p + 1, b]
                to = slice(2 * p * kxl, 2 * (p + 1) * kxl)
                lhs[2 * b, :, to] = jnp.where(half, one, two)
                lhs[2 * b + 1, :, to] = jnp.where(half, two, one)

    def grid(f, cut):
        return dot(lhs[f], (synx0 if f % 2 == 0 else synx1)[:, cut], 1, 0)

    cuts = [slice(n, n + min(256, nxp)) for n in range(0, nxp, min(256, nxp))]

    def middle_early(j):
        gather_b(j, 0, 2)
        for cut in cuts:
            for f in range(4):
                grids[f, :, cut] = grid(f, cut)

    def middle_late(j):
        gather_b(j, 2, 3)
        for cut in cuts:
            v, o = grids[2, :, cut], grids[3, :, cut]
            flux[0, :, cut] = (grids[0, :, cut] * o - v * grid(4, cut)).astype(BF)
            flux[1, :, cut] = (grids[1, :, cut] * o - v * grid(5, cut)).astype(BF)
        for t in sorted(range(nr // 2), key=lambda t: -min(t, nr // 2 - t)):
            pair = (r // 2 + t) % (nr // 2)
            cut = pl.ds(pl.multiple_of(2 * pair * kxl, 2 * kxl), 2 * kxl)
            stream_part = dot(flux[0], slopex[:, cut], 1, 0)
            span_part = dot(flux[1], anax[:, cut], 1, 0)
            send_c[j, 2 * pair] = jnp.where(half, stream_part, span_part).astype(BF)
            send_c[j, 2 * pair + 1] = jnp.where(half, span_part, stream_part).astype(BF)
            if t == 0:
                continue
            for q in (2 * pair + par, 2 * pair + 1 - par):
                remote(
                    send_c.at[j, q], recv_c.at[j, r], sc_sem.at[j], rc_sem.at[j],
                    {"px": g * nr + q, "pz": pz},
                )
        local(send_c.at[j, r], recv_c.at[j, r], rc_sem.at[j])
        q = r + 1 - 2 * par
        remote(
            send_c.at[j, q], recv_c.at[j, r], sc_sem.at[j], rc_sem.at[j],
            {"px": g * nr + q, "pz": pz},
        )

    def backward(j):
        await_all(recv_c.at[j], rc_sem.at[j])
        parts = recv_c[j].reshape(nr * zb, 2 * kxl)
        one = dot(parts, anaz[...], 0, 0)
        two = dot(parts, slopez[...], 0, 0)
        nonlinear = -jnp.where(par == 0, one[:kxl] + two[kxl:], one[kxl:] + two[:kxl])
        keep = lower[:ng]
        for c in range(QUADS):
            for p in range(npz // 2):
                cut = slice(128 * p, 128 * p + 128)
                low = nonlinear[2 * c * ng : (2 * c + 1) * ng, cut]
                high = nonlinear[(2 * c + 1) * ng : (2 * c + 2) * ng, cut]
                back[pl.ds(2 * p * ng * QUADS + c, ng, stride=QUADS), :] = jnp.where(
                    keep, low, pltpu.roll(high, KZB, 1)
                )
                back[pl.ds((2 * p + 1) * ng * QUADS + c, ng, stride=QUADS), :] = jnp.where(
                    keep, pltpu.roll(low, KZB, 1), high
                )
        send_d[j] = back[...].astype(BF).reshape(owners, QUADS, 128)

    def exchange_d(j):
        local(send_d.at[j, me], recv_d.at[j, me], rd_sem.at[j])
        each_owner(
            lambda to, device: remote(
                send_d.at[j, to], recv_d.at[j, me], sd_sem.at[j], rd_sem.at[j], device
            )
        )

    await_all(recv_a.at[0], ra_sem.at[0])
    tabs[1].wait()
    forward_early(0)
    forward_late(0)
    tabs[2].wait()
    tabs[3].wait()
    middle_early(0)
    tabs[4].wait()
    tabs[5].wait()
    middle_late(0)
    await_all(recv_a.at[1], ra_sem.at[1])
    forward_early(1)
    forward_late(1)
    tabs[6].wait()
    tabs[7].wait()
    backward(0)
    middle_early(1)
    middle_late(1)
    await_all(recv_a.at[2, :, pl.ds(0, EARLY)], ra_sem.at[2])
    forward_early(2)
    backward(1)
    await_all(recv_a.at[2, :, pl.ds(EARLY, FIELDS - EARLY)], ra_sem.at[3])
    forward_late(2)
    exchange_d(0)
    middle_early(2)
    middle_late(2)
    exchange_d(1)
    backward(2)
    exchange_d(2)

    decay = jnp.transpose(jnp.broadcast_to(decay_ref[...], (128, points)))
    lane1 = lax.broadcasted_iota(jnp.int32, (1, 128), 1)
    kz1 = SPAN_SCALE * ((KZB // 2) * pz + (lane1 % KZB) // 2).astype(F32)
    kz_square = kz1 * kz1
    for c in range(QUADS):
        lanes = slice(128 * c, 128 * c + 128)
        kx1 = STREAM_SCALE * ((KXB // 2) * px + c).astype(F32)
        rates = decay + visc_ref[0] * (kz_square + kx1 * kx1)
        denom = 1.0 + IMPLICIT * rates
        old[:, lanes] = (1.0 - EXPLICIT * rates) / denom * old[:, lanes]
        gain[:, lanes] = FORCING * dt_ref[0] / denom
    ready = owners * QUADS * (WALLS - 1)
    for j in range(WALLS - 1):
        await_all(recv_d.at[j], rd_sem.at[j])
    before = recv_d[: WALLS - 1].reshape(ready, 128)
    for c in range(QUADS):
        lanes, rows = slice(128 * c, 128 * c + 128), slice(c * points, (c + 1) * points)
        flux_coef[:, lanes] = dot(spread[rows, :ready], before, 1, 0)
    await_all(recv_d.at[WALLS - 1], rd_sem.at[WALLS - 1])
    last = recv_d[WALLS - 1].reshape(owners * QUADS, 128)
    solved = []
    for c in range(QUADS):
        lanes, rows = slice(128 * c, 128 * c + 128), slice(c * points, (c + 1) * points)
        new_coef = flux_coef[:, lanes] + dot(spread[rows, ready:], last, 1, 0)
        mixed = old[:, lanes] + gain[:, lanes] * new_coef
        solved.append(dot(basis_ref[...], mixed.astype(BF), 1, 0).astype(BF))
    result = dot(move[...], jnp.concatenate(solved, axis=1), 1, 1)
    out_ref[...] = result.astype(BF).reshape(out_ref.shape)

    for n, (j, lo, hi) in enumerate(pieces):
        await_all(send_a.at[j, pl.ds(0, owners - 1), pl.ds(lo, hi - lo)], sa_sem.at[n])
    for j in range(WALLS):
        await_all(recv_b.at[j, pl.ds(0, nr - 1), pl.ds(0, 2)], sb_sem.at[2 * j])
        await_all(recv_b.at[j, pl.ds(0, nr - 1), pl.ds(2, 1)], sb_sem.at[2 * j + 1])
        await_all(send_c.at[j, pl.ds(0, nr - 1)], sc_sem.at[j])
        await_all(send_d.at[j, pl.ds(0, owners - 1)], sd_sem.at[j])


def per_device(
    ng, nr, npz, tables,
    wall_vel, wall_slope, wall_curvature, vorticity, vort_slope,
    mean_profile, eigen_basis, eigen_decay, viscous_step, time_step,
):
    owners = ng * npz
    kxl = KXB * ng
    nkx, nkz = kxl * nr, KZB * npz
    nxp, nzp = nkx * 3 // 2, nkz * 3 // 2
    zb = nzp // nr
    points = WALLS * owners
    lanes = KZB * KXB
    hbm = pl.BlockSpec(memory_space=pltpu.HBM)
    vmem = pl.BlockSpec(memory_space=pltpu.VMEM)
    dma = pltpu.SemaphoreType.DMA
    scratch = [
        pltpu.VMEM((FIELDS, KZB, KXB, points), BF),
        *[pltpu.VMEM(t.shape, BF) for t in tables],
        pltpu.VMEM((points, points), BF),
        pltpu.VMEM((1, points), F32),
        pltpu.SMEM(mean_profile.shape, F32),
        pltpu.SMEM((1,), F32),
        pltpu.SMEM((1,), F32),
        pltpu.VMEM((WALLS * owners * FIELDS * QUADS, 128), F32),
        pltpu.VMEM((WALLS, owners, FIELDS, QUADS, 128), BF),
        pltpu.VMEM((WALLS, owners, FIELDS, QUADS, 128), BF),
        pltpu.VMEM((owners * EARLY * QUADS, 128), F32),
        pltpu.VMEM((QUADS, 4, owners, 128), F32),
        pltpu.VMEM((6 * kxl, nkz), BF),
        pltpu.VMEM((WALLS, 3, nzp, 2 * kxl), BF),
        pltpu.VMEM((WALLS, nr, 3, zb, 2 * kxl), BF),
        pltpu.VMEM((6, zb, nkx), BF),
        pltpu.VMEM((4, zb, nxp), F32),
        pltpu.VMEM((2, zb, nxp), BF),
        pltpu.VMEM((WALLS, nr, zb, 2 * kxl), BF),
        pltpu.VMEM((WALLS, nr, zb, 2 * kxl), BF),
        pltpu.VMEM((owners * QUADS, 128), F32),
        pltpu.VMEM((WALLS, owners, QUADS, 128), BF),
        pltpu.VMEM((WALLS, owners, QUADS, 128), BF),
        pltpu.VMEM((points, lanes), F32),
        pltpu.VMEM((points, lanes), F32),
        pltpu.VMEM((points, lanes), F32),
        pltpu.VMEM((points * QUADS, points * QUADS), BF),
        dma((FIELDS,)),
        dma((len(tables) + 5,)),
        *[dma((WALLS + 1,)) for _ in range(2)],
        *[dma((2 * WALLS,)) for _ in range(2)],
        *[dma((WALLS,)) for _ in range(4)],
    ]
    out = pl.pallas_call(
        functools.partial(kernel_body, ng, nr, npz),
        out_shape=pltpu.VMEM((lanes, points), BF),
        in_specs=[hbm] * (FIELDS + len(tables) + 5),
        out_specs=vmem,
        scratch_shapes=scratch,
        compiler_params=pltpu.CompilerParams(
            collective_id=0, has_side_effects=True, vmem_limit_bytes=60 * 1024 * 1024
        ),
    )(
        wall_slope, vorticity, wall_vel, wall_curvature, vort_slope,
        *[jnp.asarray(t) for t in tables],
        eigen_basis, eigen_decay.reshape(1, points), mean_profile, viscous_step, time_step,
    )
    return out.reshape(vorticity.shape)


def build(mesh, nr):
    npz = mesh.shape["pz"]
    ng = mesh.shape["px"] // nr
    tables = all_tables(ng, nr, npz)
    spec = P("pz", "px", None)
    return jax.shard_map(
        functools.partial(per_device, ng, nr, npz, tables),
        mesh=mesh,
        in_specs=(spec,) * 5 + (P(),) * 5,
        out_specs=spec,
        check_vma=False,
    )


def solution(mesh):
    return build(mesh, NR)
```

```python
import functools
import math

import jax
import jax.numpy as jnp
import ml_dtypes
import numpy as np
from jax import lax
from jax.experimental import pallas as pl
from jax.experimental.pallas import tpu as pltpu
from jax.sharding import PartitionSpec as P

NR = 8
WALLS = 3
FIELDS = 5
QUADS = 4
KZB = 64
KXB = 8

STREAM_SCALE = 0.25
SPAN_SCALE = 2.0 / 3.0
EXPLICIT = 29.0 / 96.0
IMPLICIT = 37.0 / 160.0
FORCING = 8.0 / 15.0

BF = jnp.bfloat16
F32 = jnp.float32

SLOPE, VORT, VEL, CURV, VSLOPE = range(FIELDS)
EARLY = 3


def make_tables(count, points, scale):
    indices = np.arange(count)
    number = indices // 2
    cosine = (indices % 2 == 0)[:, None]
    phase = number[:, None] * np.arange(points)[None, :] % points
    angles = phase * (2.0 * math.pi / points)
    cos_part, sin_part = np.cos(angles), np.sin(angles)
    shape_rows = np.where(cosine, cos_part, sin_part)
    norm = math.sqrt(2.0 / count)
    synthesis = norm * shape_rows
    analysis = (2.0 / points / norm * shape_rows).T
    slope_rows = np.where(cosine, sin_part, -cos_part)
    slope_analysis = ((scale * number)[:, None] * (2.0 / points / norm) * slope_rows).T

    def rounded(t):
        return t.astype(np.float32).astype(ml_dtypes.bfloat16)

    return rounded(synthesis), rounded(analysis), rounded(slope_analysis)


def all_tables(ng, nr, npz):
    kxb = KXB * ng
    nkx, nkz = kxb * nr, KZB * npz
    syn_x, ana_x, slope_x = make_tables(nkx, nkx * 3 // 2, STREAM_SCALE)
    syn_z, ana_z, slope_z = make_tables(nkz, nkz * 3 // 2, SPAN_SCALE)
    r, c, m, g = np.meshgrid(
        np.arange(nr), np.arange(QUADS), np.arange(2), np.arange(ng), indexing="ij"
    )
    order = (g * (KXB * nr) + r * KXB + 2 * c + m).reshape(nr, kxb)
    plain = order.reshape(-1)
    crossed = order.reshape(nr // 2, 2, kxb)[:, ::-1].reshape(-1)
    rows = KZB * KXB
    move = np.zeros((rows, rows), np.float32)
    kz, kx = np.meshgrid(np.arange(KZB), np.arange(KXB), indexing="ij")
    move[(kz * KXB + kx).reshape(-1), (kx * KZB + kz).reshape(-1)] = 1.0
    return (
        move.astype(ml_dtypes.bfloat16),
        np.ascontiguousarray(syn_z.T),
        np.ascontiguousarray(syn_x[plain]),
        np.ascontiguousarray(syn_x[crossed]),
        np.ascontiguousarray(slope_x[:, plain]),
        np.ascontiguousarray(ana_x[:, crossed]),
        ana_z,
        slope_z,
    )


def dot(a, b, ca, cb):
    return lax.dot_general(a, b, (((ca,), (cb,)), ((), ())), preferred_element_type=F32)


def kernel_body(
    ng, nr, npz,
    slope_h, vort_h, vel_h, curv_h, vslope_h,
    move_h, synz_h, synx0_h, synx1_h, slopex_h, anax_h, anaz_h, slopez_h,
    basis_h, decay_h, mean_h, visc_h, dt_h,
    out_ref,
    xin, move, synz, synx0, synx1, slopex, anax, anaz, slopez, basis_ref, decay_ref,
    mean_ref, visc_ref, dt_ref,
    stage, send_a, recv_a, wide, coef, mixed_rows, send_b, recv_b, lhs, grids, flux,
    send_c, recv_c, back, send_d, recv_d, old, gain, flux_coef, spread,
    in_sem, tab_sem, sa_sem, ra_sem, sb_sem, rb_sem, sc_sem, rc_sem, sd_sem, rd_sem,
):
    owners = ng * npz
    kxl = KXB * ng
    zb = synz.shape[0] // nr
    nxp = synx0.shape[1]
    points = WALLS * owners
    px = lax.axis_index("px")
    pz = lax.axis_index("pz")
    g = px // nr
    r = px % nr
    me = pz * ng + g
    par = r % 2
    ny, nz = ng // 2, 2 * npz
    y = g // 2
    z = (g % 2) * npz + pz

    def each_owner(act):
        far_first = sorted(range(ny), key=lambda dy: -min(dy, ny - dy))

        def at(dz, dy):
            z2 = (z + dz) % nz
            g2 = (y + dy) % ny * 2 + z2 // npz
            p2 = z2 % npz
            act(p2 * ng + g2, {"px": g2 * nr + r, "pz": p2})

        @pl.loop(0, nz - 1)
        def _(k):
            up, down = nz // 2 + (k + 1) // 2, nz // 2 - k // 2
            dz = k % 2 * up + (1 - k % 2) * down
            for dy in far_first:
                at(dz, dy)

        for dy in far_first[:-1]:
            at(0, dy)

    def each_peer(act):
        for t in sorted(range(1, nr), key=lambda t: -min(t, nr - t)):
            q = (r + t) % nr
            act(q, {"px": g * nr + q, "pz": pz})

    def remote(src, dst, send_sem, recv_sem, device):
        pltpu.make_async_remote_copy(
            src_ref=src, dst_ref=dst, send_sem=send_sem, recv_sem=recv_sem,
            device_id=device, device_id_type=pl.DeviceIdType.MESH,
        ).start()

    def local(src, dst, sem):
        pltpu.make_async_copy(src, dst, sem).start()

    def await_all(ref, sem):
        pltpu.make_async_copy(ref, ref, sem).wait()

    barrier = pltpu.get_barrier_semaphore()

    def greet(_, device):
        pl.semaphore_signal(
            barrier, inc=1, device_id=device, device_id_type=pl.DeviceIdType.MESH
        )

    each_owner(greet)
    each_peer(greet)

    tabs = [
        pltpu.make_async_copy(h, v, tab_sem.at[i])
        for i, (h, v) in enumerate(
            (
                (move_h, move), (synz_h, synz), (synx0_h, synx0), (synx1_h, synx1),
                (slopex_h, slopex), (anax_h, anax), (anaz_h, anaz), (slopez_h, slopez),
                (basis_h, basis_ref), (decay_h, decay_ref),
                (mean_h, mean_ref), (visc_h, visc_ref), (dt_h, dt_ref),
            )
        )
    ]
    ins = [
        pltpu.make_async_copy(h, xin.at[i], in_sem.at[i])
        for i, h in enumerate((slope_h, vort_h, vel_h, curv_h, vslope_h))
    ]
    tabs[0].start()
    for copy in ins:
        copy.start()

    tabs[0].wait()
    per_owner = FIELDS * QUADS
    for i in range(FIELDS):
        ins[i].wait()
        block = xin[i].reshape(KZB * KXB, points)
        turned = dot(block, move[...], 0, 0)
        for j in range(WALLS):
            for c in range(QUADS):
                stage[pl.ds(j * owners * per_owner + i * QUADS + c, owners, stride=per_owner), :] = (
                    turned[j * owners : (j + 1) * owners, 128 * c : 128 * c + 128]
                )
        if i == VORT:
            old[...] = turned

    for copy in tabs[8:] + tabs[1:8]:
        copy.start()

    pieces = [(j, 0, FIELDS) for j in range(WALLS - 1)]
    pieces += [(WALLS - 1, 0, EARLY), (WALLS - 1, EARLY, FIELDS)]
    for n, (j, lo, hi) in enumerate(pieces):
        if lo == 0:
            rows = owners * per_owner
            send_a[j] = (
                stage[j * rows : (j + 1) * rows, :].astype(BF).reshape(owners, FIELDS, QUADS, 128)
            )
        if n == 0:
            pl.semaphore_wait(barrier, owners - 1 + nr - 1)
        part = pl.ds(lo, hi - lo)
        local(send_a.at[j, me, part], recv_a.at[j, me, part], ra_sem.at[n])

        def send(to, device, n=n, j=j, part=part):
            remote(
                send_a.at[j, to, part], recv_a.at[j, me, part], sa_sem.at[n], ra_sem.at[n], device
            )

        each_owner(send)

    row = lax.broadcasted_iota(jnp.int32, (owners, 128), 0)
    lane = lax.broadcasted_iota(jnp.int32, (owners, 128), 1)
    lower = lane < KZB
    even = lane % 2 == 0
    kz_rate = SPAN_SCALE * ((KZB // 2) * (row // ng) + (lane % KZB) // 2).astype(F32)
    fz = jnp.where(even, kz_rate, -kz_rate)
    for c in range(QUADS):
        number = (KXB // 2) * nr * (row % ng) + (KXB // 2) * r + c
        kx_rate = STREAM_SCALE * number.astype(F32)
        fx = jnp.where(lower, kx_rate, -kx_rate)
        square = kx_rate * kx_rate + kz_rate * kz_rate
        safe = jnp.where(square == 0.0, 1.0, square)
        coef[c, 0] = fx
        coef[c, 1] = fx / safe
        coef[c, 2] = fz / safe
    coef[0, 3] = fz

    for copy in tabs[8:]:
        copy.wait()
    col = lax.broadcasted_iota(jnp.int32, (points, points * QUADS), 1)
    point = lax.broadcasted_iota(jnp.int32, (points, points * QUADS), 0)
    wide_basis = dot(
        basis_ref[...], jnp.where(col // QUADS == point, 1.0, 0.0).astype(BF), 0, 0
    )
    for c in range(QUADS):
        spread[c * points : (c + 1) * points, :] = jnp.where(
            col % QUADS == c, wide_basis, 0.0
        ).astype(BF)
    old[...] = dot(basis_ref[...], old[...].astype(BF), 0, 0)

    def swap_x(v):
        return pltpu.roll(v, KZB, 1)

    def swap_z(v):
        return jnp.where(even, pltpu.roll(v, 127, 1), pltpu.roll(v, 1, 1))

    first = (row == 0) & (lane == 0) & (r == 0)

    def unpack(j, lo, hi):
        rows = (hi - lo) * QUADS
        wide[0 : owners * rows, :] = (
            recv_a[j, :, lo:hi].reshape(owners * rows, 128).astype(F32)
        )
        return lambda i, c: wide[pl.ds((i - lo) * QUADS + c, owners, stride=rows), :]

    def place(f, c, field):
        at = pl.multiple_of((f + par - 2 * par * (f % 2)) * kxl + c * 2 * ng, 2 * ng)
        keep = lower[:ng]
        low, high = [], []
        for p in range(npz // 2):
            one = field[2 * p * ng : (2 * p + 1) * ng]
            two = field[(2 * p + 1) * ng : (2 * p + 2) * ng]
            low.append(jnp.where(keep, one, pltpu.roll(two, KZB, 1)))
            high.append(jnp.where(keep, pltpu.roll(one, KZB, 1), two))
        packed = jnp.concatenate(
            [jnp.concatenate(low, axis=1), jnp.concatenate(high, axis=1)], axis=0
        )
        mixed_rows[pl.ds(at, 2 * ng), :] = packed.astype(BF)

    def exchange_b(j, lo, hi):
        width = 2 * kxl
        made = dot(synz[...], mixed_rows[lo * width : hi * width, :], 1, 1).astype(BF)
        for b in range(lo, hi):
            send_b[j, b] = made[:, (b - lo) * width : (b - lo + 1) * width]
        part = pl.ds(lo, hi - lo)
        n = 2 * j + (lo > 0)

        def rows(q):
            return send_b.at[j, part, pl.ds(pl.multiple_of(q * zb, zb), zb)]

        local(rows(r), recv_b.at[j, r, part], rb_sem.at[n])
        each_peer(
            lambda q, device: remote(
                rows(q), recv_b.at[j, r, part], sb_sem.at[n], rb_sem.at[n], device
            )
        )

    def mean(i, j):
        return jnp.where(first, mean_ref[i, owners * j + me], 0.0)

    def forward_early(j):
        load = unpack(j, 0, EARLY)
        for c in range(QUADS):
            s, o, v = load(SLOPE, c), load(VORT, c), load(VEL, c)
            a, b = coef[c, 1], coef[c, 2]
            stream_vel = swap_z(b * o) - swap_x(a * s)
            span_vel = -swap_z(b * s) - swap_x(a * o)
            if c == 0:
                stream_vel += mean(0, j)
                span_vel += mean(1, j)
            for f, field in enumerate((stream_vel, span_vel, v, o)):
                place(f, c, field)
        exchange_b(j, 0, 2)

    def forward_late(j):
        load = unpack(j, VEL, FIELDS)
        for c in range(QUADS):
            v, cv, q = load(VEL, c), load(CURV, c), load(VSLOPE, c)
            fx, a, b, fzz = coef[c, 0], coef[c, 1], coef[c, 2], coef[0, 3]
            stream_vort = swap_z(fzz * v - b * cv) - swap_x(a * q)
            span_vort = swap_x(a * cv - fx * v) - swap_z(b * q)
            if c == 0:
                stream_vort += mean(3, j)
                span_vort -= mean(2, j)
            place(4, c, stream_vort)
            place(5, c, span_vort)
        exchange_b(j, 2, 3)

    half = lax.broadcasted_iota(jnp.int32, (zb, 2 * kxl), 1) < kxl

    def gather_b(j, lo, hi):
        await_all(recv_b.at[j, :, pl.ds(lo, hi - lo)], rb_sem.at[2 * j + (lo > 0)])
        for b in range(lo, hi):
            for p in range(nr // 2):
                one, two = recv_b[j, 2 * p, b], recv_b[j, 2 * p + 1, b]
                to = slice(2 * p * kxl, 2 * (p + 1) * kxl)
                lhs[2 * b, :, to] = jnp.where(half, one, two)
                lhs[2 * b + 1, :, to] = jnp.where(half, two, one)

    def grid(f, cut):
        return dot(lhs[f], (synx0 if f % 2 == 0 else synx1)[:, cut], 1, 0)

    cuts = [slice(n, n + min(256, nxp)) for n in range(0, nxp, min(256, nxp))]

    def middle_early(j):
        gather_b(j, 0, 2)
        for cut in cuts:
            for f in range(4):
                grids[f, :, cut] = grid(f, cut)

    def exchange_c(j, q):
        remote(
            send_c.at[j, q], recv_c.at[j, r], sc_sem.at[j], rc_sem.at[j],
            {"px": g * nr + q, "pz": pz},
        )

    def middle_late(j, held=False):
        gather_b(j, 2, 3)
        for cut in cuts:
            v, o = grids[2, :, cut], grids[3, :, cut]
            flux[0, :, cut] = (grids[0, :, cut] * o - v * grid(4, cut)).astype(BF)
            flux[1, :, cut] = (grids[1, :, cut] * o - v * grid(5, cut)).astype(BF)
        for t in sorted(range(nr // 2), key=lambda t: -min(t, nr // 2 - t)):
            pair = (r // 2 + t) % (nr // 2)
            cut = pl.ds(pl.multiple_of(2 * pair * kxl, 2 * kxl), 2 * kxl)
            stream_part = dot(flux[0], slopex[:, cut], 1, 0)
            span_part = dot(flux[1], anax[:, cut], 1, 0)
            send_c[j, 2 * pair] = jnp.where(half, stream_part, span_part).astype(BF)
            send_c[j, 2 * pair + 1] = jnp.where(half, span_part, stream_part).astype(BF)
            if t > 0 and not held:
                exchange_c(j, 2 * pair + par)
                exchange_c(j, 2 * pair + 1 - par)
        local(send_c.at[j, r], recv_c.at[j, r], rc_sem.at[j])
        if not held:
            exchange_c(j, r + 1 - 2 * par)

    def backward(j):
        await_all(recv_c.at[j], rc_sem.at[j])
        parts = recv_c[j].reshape(nr * zb, 2 * kxl)
        one = dot(parts, anaz[...], 0, 0)
        two = dot(parts, slopez[...], 0, 0)
        nonlinear = -jnp.where(par == 0, one[:kxl] + two[kxl:], one[kxl:] + two[:kxl])
        keep = lower[:ng]
        for c in range(QUADS):
            for p in range(npz // 2):
                cut = slice(128 * p, 128 * p + 128)
                low = nonlinear[2 * c * ng : (2 * c + 1) * ng, cut]
                high = nonlinear[(2 * c + 1) * ng : (2 * c + 2) * ng, cut]
                back[pl.ds(2 * p * ng * QUADS + c, ng, stride=QUADS), :] = jnp.where(
                    keep, low, pltpu.roll(high, KZB, 1)
                )
                back[pl.ds((2 * p + 1) * ng * QUADS + c, ng, stride=QUADS), :] = jnp.where(
                    keep, pltpu.roll(low, KZB, 1), high
                )
        send_d[j] = back[...].astype(BF).reshape(owners, QUADS, 128)

    def exchange_d(j):
        local(send_d.at[j, me], recv_d.at[j, me], rd_sem.at[j])
        each_owner(
            lambda to, device: remote(
                send_d.at[j, to], recv_d.at[j, me], sd_sem.at[j], rd_sem.at[j], device
            )
        )

    await_all(recv_a.at[0], ra_sem.at[0])
    tabs[1].wait()
    forward_early(0)
    forward_late(0)
    tabs[2].wait()
    tabs[3].wait()
    middle_early(0)
    tabs[4].wait()
    tabs[5].wait()
    middle_late(0)
    await_all(recv_a.at[1], ra_sem.at[1])
    forward_early(1)
    forward_late(1)
    tabs[6].wait()
    tabs[7].wait()
    backward(0)
    await_all(recv_a.at[2, :, pl.ds(0, EARLY)], ra_sem.at[2])
    forward_early(2)
    middle_early(1)
    middle_late(1, held=True)
    await_all(recv_a.at[2, :, pl.ds(EARLY, FIELDS - EARLY)], ra_sem.at[3])
    forward_late(2)
    each_peer(lambda q, _: exchange_c(1, q))
    exchange_d(0)
    middle_early(2)
    middle_late(2)
    backward(1)
    exchange_d(1)
    backward(2)
    exchange_d(2)

    decay = jnp.transpose(jnp.broadcast_to(decay_ref[...], (128, points)))
    lane1 = lax.broadcasted_iota(jnp.int32, (1, 128), 1)
    kz1 = SPAN_SCALE * ((KZB // 2) * pz + (lane1 % KZB) // 2).astype(F32)
    kz_square = kz1 * kz1
    for c in range(QUADS):
        lanes = slice(128 * c, 128 * c + 128)
        kx1 = STREAM_SCALE * ((KXB // 2) * px + c).astype(F32)
        rates = decay + visc_ref[0] * (kz_square + kx1 * kx1)
        denom = 1.0 + IMPLICIT * rates
        old[:, lanes] = (1.0 - EXPLICIT * rates) / denom * old[:, lanes]
        gain[:, lanes] = FORCING * dt_ref[0] / denom
    ready = owners * QUADS * (WALLS - 1)
    for j in range(WALLS - 1):
        await_all(recv_d.at[j], rd_sem.at[j])
    before = recv_d[: WALLS - 1].reshape(ready, 128)
    for c in range(QUADS):
        lanes, rows = slice(128 * c, 128 * c + 128), slice(c * points, (c + 1) * points)
        flux_coef[:, lanes] = dot(spread[rows, :ready], before, 1, 0)
    await_all(recv_d.at[WALLS - 1], rd_sem.at[WALLS - 1])
    last = recv_d[WALLS - 1].reshape(owners * QUADS, 128)
    solved = []
    for c in range(QUADS):
        lanes, rows = slice(128 * c, 128 * c + 128), slice(c * points, (c + 1) * points)
        new_coef = flux_coef[:, lanes] + dot(spread[rows, ready:], last, 1, 0)
        mixed = old[:, lanes] + gain[:, lanes] * new_coef
        solved.append(dot(basis_ref[...], mixed.astype(BF), 1, 0).astype(BF))
    result = dot(move[...], jnp.concatenate(solved, axis=1), 1, 1)
    out_ref[...] = result.astype(BF).reshape(out_ref.shape)

    for n, (j, lo, hi) in enumerate(pieces):
        await_all(send_a.at[j, pl.ds(0, owners - 1), pl.ds(lo, hi - lo)], sa_sem.at[n])
    for j in range(WALLS):
        await_all(recv_b.at[j, pl.ds(0, nr - 1), pl.ds(0, 2)], sb_sem.at[2 * j])
        await_all(recv_b.at[j, pl.ds(0, nr - 1), pl.ds(2, 1)], sb_sem.at[2 * j + 1])
        await_all(send_c.at[j, pl.ds(0, nr - 1)], sc_sem.at[j])
        await_all(send_d.at[j, pl.ds(0, owners - 1)], sd_sem.at[j])


def per_device(
    ng, nr, npz, tables,
    wall_vel, wall_slope, wall_curvature, vorticity, vort_slope,
    mean_profile, eigen_basis, eigen_decay, viscous_step, time_step,
):
    owners = ng * npz
    kxl = KXB * ng
    nkx, nkz = kxl * nr, KZB * npz
    nxp, nzp = nkx * 3 // 2, nkz * 3 // 2
    zb = nzp // nr
    points = WALLS * owners
    lanes = KZB * KXB
    hbm = pl.BlockSpec(memory_space=pltpu.HBM)
    vmem = pl.BlockSpec(memory_space=pltpu.VMEM)
    dma = pltpu.SemaphoreType.DMA
    scratch = [
        pltpu.VMEM((FIELDS, KZB, KXB, points), BF),
        *[pltpu.VMEM(t.shape, BF) for t in tables],
        pltpu.VMEM((points, points), BF),
        pltpu.VMEM((1, points), F32),
        pltpu.SMEM(mean_profile.shape, F32),
        pltpu.SMEM((1,), F32),
        pltpu.SMEM((1,), F32),
        pltpu.VMEM((WALLS * owners * FIELDS * QUADS, 128), F32),
        pltpu.VMEM((WALLS, owners, FIELDS, QUADS, 128), BF),
        pltpu.VMEM((WALLS, owners, FIELDS, QUADS, 128), BF),
        pltpu.VMEM((owners * EARLY * QUADS, 128), F32),
        pltpu.VMEM((QUADS, 4, owners, 128), F32),
        pltpu.VMEM((6 * kxl, nkz), BF),
        pltpu.VMEM((WALLS, 3, nzp, 2 * kxl), BF),
        pltpu.VMEM((WALLS, nr, 3, zb, 2 * kxl), BF),
        pltpu.VMEM((6, zb, nkx), BF),
        pltpu.VMEM((4, zb, nxp), F32),
        pltpu.VMEM((2, zb, nxp), BF),
        pltpu.VMEM((WALLS, nr, zb, 2 * kxl), BF),
        pltpu.VMEM((WALLS, nr, zb, 2 * kxl), BF),
        pltpu.VMEM((owners * QUADS, 128), F32),
        pltpu.VMEM((WALLS, owners, QUADS, 128), BF),
        pltpu.VMEM((WALLS, owners, QUADS, 128), BF),
        pltpu.VMEM((points, lanes), F32),
        pltpu.VMEM((points, lanes), F32),
        pltpu.VMEM((points, lanes), F32),
        pltpu.VMEM((points * QUADS, points * QUADS), BF),
        dma((FIELDS,)),
        dma((len(tables) + 5,)),
        *[dma((WALLS + 1,)) for _ in range(2)],
        *[dma((2 * WALLS,)) for _ in range(2)],
        *[dma((WALLS,)) for _ in range(4)],
    ]
    out = pl.pallas_call(
        functools.partial(kernel_body, ng, nr, npz),
        out_shape=pltpu.VMEM((lanes, points), BF),
        in_specs=[hbm] * (FIELDS + len(tables) + 5),
        out_specs=vmem,
        scratch_shapes=scratch,
        compiler_params=pltpu.CompilerParams(
            collective_id=0, has_side_effects=True, vmem_limit_bytes=60 * 1024 * 1024
        ),
    )(
        wall_slope, vorticity, wall_vel, wall_curvature, vort_slope,
        *[jnp.asarray(t) for t in tables],
        eigen_basis, eigen_decay.reshape(1, points), mean_profile, viscous_step, time_step,
    )
    return out.reshape(vorticity.shape)


def build(mesh, nr):
    npz = mesh.shape["pz"]
    ng = mesh.shape["px"] // nr
    tables = all_tables(ng, nr, npz)
    spec = P("pz", "px", None)
    return jax.shard_map(
        functools.partial(per_device, ng, nr, npz, tables),
        mesh=mesh,
        in_specs=(spec,) * 5 + (P(),) * 5,
        out_specs=spec,
        check_vma=False,
    )


def solution(mesh):
    return build(mesh, NR)
```

```python
import functools
import math

import jax
import jax.numpy as jnp
import ml_dtypes
import numpy as np
from jax import lax
from jax.experimental import pallas as pl
from jax.experimental.pallas import tpu as pltpu
from jax.sharding import PartitionSpec as P

NR = 8
WALLS = 3
FIELDS = 5
QUADS = 4
KZB = 64
KXB = 8

STREAM_SCALE = 0.25
SPAN_SCALE = 2.0 / 3.0
EXPLICIT = 29.0 / 96.0
IMPLICIT = 37.0 / 160.0
FORCING = 8.0 / 15.0

BF = jnp.bfloat16
F32 = jnp.float32

SLOPE, VORT, VEL, CURV, VSLOPE = range(FIELDS)
EARLY = 3


def make_tables(count, points, scale):
    indices = np.arange(count)
    number = indices // 2
    cosine = (indices % 2 == 0)[:, None]
    phase = number[:, None] * np.arange(points)[None, :] % points
    angles = phase * (2.0 * math.pi / points)
    cos_part, sin_part = np.cos(angles), np.sin(angles)
    shape_rows = np.where(cosine, cos_part, sin_part)
    norm = math.sqrt(2.0 / count)
    synthesis = norm * shape_rows
    analysis = (2.0 / points / norm * shape_rows).T
    slope_rows = np.where(cosine, sin_part, -cos_part)
    slope_analysis = ((scale * number)[:, None] * (2.0 / points / norm) * slope_rows).T

    def rounded(t):
        return t.astype(np.float32).astype(ml_dtypes.bfloat16)

    return rounded(synthesis), rounded(analysis), rounded(slope_analysis)


def all_tables(ng, nr, npz):
    kxb = KXB * ng
    nkx, nkz = kxb * nr, KZB * npz
    syn_x, ana_x, slope_x = make_tables(nkx, nkx * 3 // 2, STREAM_SCALE)
    syn_z, ana_z, slope_z = make_tables(nkz, nkz * 3 // 2, SPAN_SCALE)
    r, c, m, g = np.meshgrid(
        np.arange(nr), np.arange(QUADS), np.arange(2), np.arange(ng), indexing="ij"
    )
    order = (g * (KXB * nr) + r * KXB + 2 * c + m).reshape(nr, kxb)
    plain = order.reshape(-1)
    crossed = order.reshape(nr // 2, 2, kxb)[:, ::-1].reshape(-1)
    rows = KZB * KXB
    move = np.zeros((rows, rows), np.float32)
    kz, kx = np.meshgrid(np.arange(KZB), np.arange(KXB), indexing="ij")
    move[(kz * KXB + kx).reshape(-1), (kx * KZB + kz).reshape(-1)] = 1.0
    return (
        move.astype(ml_dtypes.bfloat16),
        np.ascontiguousarray(syn_z.T),
        np.ascontiguousarray(syn_x[plain]),
        np.ascontiguousarray(syn_x[crossed]),
        np.ascontiguousarray(slope_x[:, plain]),
        np.ascontiguousarray(ana_x[:, crossed]),
        ana_z,
        slope_z,
    )


def dot(a, b, ca, cb):
    return lax.dot_general(a, b, (((ca,), (cb,)), ((), ())), preferred_element_type=F32)


def kernel_body(
    ng, nr, npz,
    slope_h, vort_h, vel_h, curv_h, vslope_h,
    move_h, synz_h, synx0_h, synx1_h, slopex_h, anax_h, anaz_h, slopez_h,
    basis_h, decay_h, mean_h, visc_h, dt_h,
    out_ref,
    xin, move, synz, synx0, synx1, slopex, anax, anaz, slopez, basis_ref, decay_ref,
    mean_ref, visc_ref, dt_ref,
    stage, send_a, recv_a, wide, coef, mixed_rows, send_b, recv_b, lhs, grids, flux,
    send_c, recv_c, back, send_d, recv_d, old, gain, flux_coef, spread,
    in_sem, tab_sem, sa_sem, ra_sem, sb_sem, rb_sem, sc_sem, rc_sem, sd_sem, rd_sem,
):
    owners = ng * npz
    kxl = KXB * ng
    zb = synz.shape[0] // nr
    nxp = synx0.shape[1]
    points = WALLS * owners
    px = lax.axis_index("px")
    pz = lax.axis_index("pz")
    g = px // nr
    r = px % nr
    me = pz * ng + g
    par = r % 2
    ny, nz = ng // 2, 2 * npz
    y = g // 2
    z = (g % 2) * npz + pz
    rows_g = [lax.rem(y + dy, ny) * 2 for dy in range(ny)]

    def each_owner(act):
        far_first = sorted(range(ny), key=lambda dy: -min(dy, ny - dy))

        def at(dz, dys):
            z2 = lax.rem(z + dz, nz)
            high = lax.div(z2, npz)
            p2 = z2 - high * npz
            to = p2 * ng + high
            place = high * nr + r
            for dy in dys:
                act(to + rows_g[dy], {"px": place + rows_g[dy] * nr, "pz": p2})

        @pl.loop(0, nz - 1)
        def _(k):
            half = lax.div(k + 1, 2)
            up = half + half - k
            at(nz // 2 + up * half - (1 - up) * half, far_first)

        at(0, far_first[:-1])

    def each_peer(act):
        for t in sorted(range(1, nr), key=lambda t: -min(t, nr - t)):
            q = lax.rem(r + t, nr)
            act(q, {"px": g * nr + q, "pz": pz})

    def remote(src, dst, send_sem, recv_sem, device):
        pltpu.make_async_remote_copy(
            src_ref=src, dst_ref=dst, send_sem=send_sem, recv_sem=recv_sem,
            device_id=device, device_id_type=pl.DeviceIdType.MESH,
        ).start()

    def local(src, dst, sem):
        pltpu.make_async_copy(src, dst, sem).start()

    def await_all(ref, sem):
        pltpu.make_async_copy(ref, ref, sem).wait()

    barrier = pltpu.get_barrier_semaphore()

    def greet(_, device):
        pl.semaphore_signal(
            barrier, inc=1, device_id=device, device_id_type=pl.DeviceIdType.MESH
        )

    each_owner(greet)
    each_peer(greet)

    tabs = [
        pltpu.make_async_copy(h, v, tab_sem.at[i])
        for i, (h, v) in enumerate(
            (
                (move_h, move), (synz_h, synz), (synx0_h, synx0), (synx1_h, synx1),
                (slopex_h, slopex), (anax_h, anax), (anaz_h, anaz), (slopez_h, slopez),
                (basis_h, basis_ref), (decay_h, decay_ref),
                (mean_h, mean_ref), (visc_h, visc_ref), (dt_h, dt_ref),
            )
        )
    ]
    ins = [
        pltpu.make_async_copy(h, xin.at[i], in_sem.at[i])
        for i, h in enumerate((slope_h, vort_h, vel_h, curv_h, vslope_h))
    ]
    tabs[0].start()
    for copy in ins:
        copy.start()

    tabs[0].wait()
    per_owner = FIELDS * QUADS
    for i in range(FIELDS):
        ins[i].wait()
        block = xin[i].reshape(KZB * KXB, points)
        turned = dot(block, move[...], 0, 0)
        for j in range(WALLS):
            for c in range(QUADS):
                stage[pl.ds(j * owners * per_owner + i * QUADS + c, owners, stride=per_owner), :] = (
                    turned[j * owners : (j + 1) * owners, 128 * c : 128 * c + 128]
                )
        if i == VORT:
            old[...] = turned

    for copy in tabs[8:] + tabs[1:8]:
        copy.start()

    pieces = [(j, 0, FIELDS) for j in range(WALLS - 1)]
    pieces += [(WALLS - 1, 0, EARLY), (WALLS - 1, EARLY, FIELDS)]
    for n, (j, lo, hi) in enumerate(pieces):
        if lo == 0:
            rows = owners * per_owner
            send_a[j] = (
                stage[j * rows : (j + 1) * rows, :].astype(BF).reshape(owners, FIELDS, QUADS, 128)
            )
        if n == 0:
            pl.semaphore_wait(barrier, owners - 1 + nr - 1)
        part = pl.ds(lo, hi - lo)
        local(send_a.at[j, me, part], recv_a.at[j, me, part], ra_sem.at[n])

        def send(to, device, n=n, j=j, part=part):
            remote(
                send_a.at[j, to, part], recv_a.at[j, me, part], sa_sem.at[n], ra_sem.at[n], device
            )

        each_owner(send)

    row = lax.broadcasted_iota(jnp.int32, (owners, 128), 0)
    lane = lax.broadcasted_iota(jnp.int32, (owners, 128), 1)
    lower = lane < KZB
    even = lane % 2 == 0
    kz_rate = SPAN_SCALE * ((KZB // 2) * (row // ng) + (lane % KZB) // 2).astype(F32)
    fz = jnp.where(even, kz_rate, -kz_rate)
    for c in range(QUADS):
        number = (KXB // 2) * nr * (row % ng) + (KXB // 2) * r + c
        kx_rate = STREAM_SCALE * number.astype(F32)
        fx = jnp.where(lower, kx_rate, -kx_rate)
        square = kx_rate * kx_rate + kz_rate * kz_rate
        safe = jnp.where(square == 0.0, 1.0, square)
        coef[c, 0] = fx
        coef[c, 1] = fx / safe
        coef[c, 2] = fz / safe
    coef[0, 3] = fz

    for copy in tabs[8:]:
        copy.wait()
    col = lax.broadcasted_iota(jnp.int32, (points, points * QUADS), 1)
    point = lax.broadcasted_iota(jnp.int32, (points, points * QUADS), 0)
    wide_basis = dot(
        basis_ref[...], jnp.where(col // QUADS == point, 1.0, 0.0).astype(BF), 0, 0
    )
    for c in range(QUADS):
        spread[c * points : (c + 1) * points, :] = jnp.where(
            col % QUADS == c, wide_basis, 0.0
        ).astype(BF)
    old[...] = dot(basis_ref[...], old[...].astype(BF), 0, 0)

    def swap_x(v):
        return pltpu.roll(v, KZB, 1)

    def swap_z(v):
        return jnp.where(even, pltpu.roll(v, 127, 1), pltpu.roll(v, 1, 1))

    first = (row == 0) & (lane == 0) & (r == 0)

    def unpack(j, lo, hi):
        rows = (hi - lo) * QUADS
        wide[0 : owners * rows, :] = (
            recv_a[j, :, lo:hi].reshape(owners * rows, 128).astype(F32)
        )
        return lambda i, c: wide[pl.ds((i - lo) * QUADS + c, owners, stride=rows), :]

    def place(f, c, field):
        at = pl.multiple_of((f + par - 2 * par * (f % 2)) * kxl + c * 2 * ng, 2 * ng)
        keep = lower[:ng]
        low, high = [], []
        for p in range(npz // 2):
            one = field[2 * p * ng : (2 * p + 1) * ng]
            two = field[(2 * p + 1) * ng : (2 * p + 2) * ng]
            low.append(jnp.where(keep, one, pltpu.roll(two, KZB, 1)))
            high.append(jnp.where(keep, pltpu.roll(one, KZB, 1), two))
        packed = jnp.concatenate(
            [jnp.concatenate(low, axis=1), jnp.concatenate(high, axis=1)], axis=0
        )
        mixed_rows[pl.ds(at, 2 * ng), :] = packed.astype(BF)

    def exchange_b(j, lo, hi):
        width = 2 * kxl
        made = dot(synz[...], mixed_rows[lo * width : hi * width, :], 1, 1).astype(BF)
        for b in range(lo, hi):
            send_b[j, b] = made[:, (b - lo) * width : (b - lo + 1) * width]
        part = pl.ds(lo, hi - lo)
        n = 2 * j + (lo > 0)

        def rows(q):
            return send_b.at[j, part, pl.ds(pl.multiple_of(q * zb, zb), zb)]

        local(rows(r), recv_b.at[j, r, part], rb_sem.at[n])
        each_peer(
            lambda q, device: remote(
                rows(q), recv_b.at[j, r, part], sb_sem.at[n], rb_sem.at[n], device
            )
        )

    def mean(i, j):
        return jnp.where(first, mean_ref[i, owners * j + me], 0.0)

    def forward_early(j):
        load = unpack(j, 0, EARLY)
        for c in range(QUADS):
            s, o, v = load(SLOPE, c), load(VORT, c), load(VEL, c)
            a, b = coef[c, 1], coef[c, 2]
            stream_vel = swap_z(b * o) - swap_x(a * s)
            span_vel = -swap_z(b * s) - swap_x(a * o)
            if c == 0:
                stream_vel += mean(0, j)
                span_vel += mean(1, j)
            for f, field in enumerate((stream_vel, span_vel, v, o)):
                place(f, c, field)
        exchange_b(j, 0, 2)

    def forward_late(j):
        load = unpack(j, VEL, FIELDS)
        for c in range(QUADS):
            v, cv, q = load(VEL, c), load(CURV, c), load(VSLOPE, c)
            fx, a, b, fzz = coef[c, 0], coef[c, 1], coef[c, 2], coef[0, 3]
            stream_vort = swap_z(fzz * v - b * cv) - swap_x(a * q)
            span_vort = swap_x(a * cv - fx * v) - swap_z(b * q)
            if c == 0:
                stream_vort += mean(3, j)
                span_vort -= mean(2, j)
            place(4, c, stream_vort)
            place(5, c, span_vort)
        exchange_b(j, 2, 3)

    half = lax.broadcasted_iota(jnp.int32, (zb, 2 * kxl), 1) < kxl

    def gather_b(j, lo, hi):
        await_all(recv_b.at[j, :, pl.ds(lo, hi - lo)], rb_sem.at[2 * j + (lo > 0)])
        for b in range(lo, hi):
            for p in range(nr // 2):
                one, two = recv_b[j, 2 * p, b], recv_b[j, 2 * p + 1, b]
                to = slice(2 * p * kxl, 2 * (p + 1) * kxl)
                lhs[2 * b, :, to] = jnp.where(half, one, two)
                lhs[2 * b + 1, :, to] = jnp.where(half, two, one)

    def grid(f, cut):
        return dot(lhs[f], (synx0 if f % 2 == 0 else synx1)[:, cut], 1, 0)

    cuts = [slice(n, n + min(256, nxp)) for n in range(0, nxp, min(256, nxp))]

    def middle_early(j):
        gather_b(j, 0, 2)
        for cut in cuts:
            for f in range(4):
                grids[f, :, cut] = grid(f, cut)

    def exchange_c(j, q):
        remote(
            send_c.at[j, q], recv_c.at[j, r], sc_sem.at[j], rc_sem.at[j],
            {"px": g * nr + q, "pz": pz},
        )

    def middle_late(j, held=False):
        gather_b(j, 2, 3)
        for cut in cuts:
            v, o = grids[2, :, cut], grids[3, :, cut]
            flux[0, :, cut] = (grids[0, :, cut] * o - v * grid(4, cut)).astype(BF)
            flux[1, :, cut] = (grids[1, :, cut] * o - v * grid(5, cut)).astype(BF)
        for t in sorted(range(nr // 2), key=lambda t: -min(t, nr // 2 - t)):
            pair = (r // 2 + t) % (nr // 2)
            cut = pl.ds(pl.multiple_of(2 * pair * kxl, 2 * kxl), 2 * kxl)
            stream_part = dot(flux[0], slopex[:, cut], 1, 0)
            span_part = dot(flux[1], anax[:, cut], 1, 0)
            send_c[j, 2 * pair] = jnp.where(half, stream_part, span_part).astype(BF)
            send_c[j, 2 * pair + 1] = jnp.where(half, span_part, stream_part).astype(BF)
            if t > 0 and not held:
                exchange_c(j, 2 * pair + par)
                exchange_c(j, 2 * pair + 1 - par)
        local(send_c.at[j, r], recv_c.at[j, r], rc_sem.at[j])
        if not held:
            exchange_c(j, r + 1 - 2 * par)

    def backward(j):
        await_all(recv_c.at[j], rc_sem.at[j])
        parts = recv_c[j].reshape(nr * zb, 2 * kxl)
        one = dot(parts, anaz[...], 0, 0)
        two = dot(parts, slopez[...], 0, 0)
        nonlinear = -jnp.where(par == 0, one[:kxl] + two[kxl:], one[kxl:] + two[:kxl])
        keep = lower[:ng]
        for c in range(QUADS):
            for p in range(npz // 2):
                cut = slice(128 * p, 128 * p + 128)
                low = nonlinear[2 * c * ng : (2 * c + 1) * ng, cut]
                high = nonlinear[(2 * c + 1) * ng : (2 * c + 2) * ng, cut]
                back[pl.ds(2 * p * ng * QUADS + c, ng, stride=QUADS), :] = jnp.where(
                    keep, low, pltpu.roll(high, KZB, 1)
                )
                back[pl.ds((2 * p + 1) * ng * QUADS + c, ng, stride=QUADS), :] = jnp.where(
                    keep, pltpu.roll(low, KZB, 1), high
                )
        send_d[j] = back[...].astype(BF).reshape(owners, QUADS, 128)

    def exchange_d(j):
        local(send_d.at[j, me], recv_d.at[j, me], rd_sem.at[j])
        each_owner(
            lambda to, device: remote(
                send_d.at[j, to], recv_d.at[j, me], sd_sem.at[j], rd_sem.at[j], device
            )
        )

    await_all(recv_a.at[0], ra_sem.at[0])
    tabs[1].wait()
    forward_early(0)
    forward_late(0)
    tabs[2].wait()
    tabs[3].wait()
    middle_early(0)
    tabs[4].wait()
    tabs[5].wait()
    middle_late(0)
    await_all(recv_a.at[1], ra_sem.at[1])
    forward_early(1)
    forward_late(1)
    tabs[6].wait()
    tabs[7].wait()
    backward(0)
    await_all(recv_a.at[2, :, pl.ds(0, EARLY)], ra_sem.at[2])
    forward_early(2)
    middle_early(1)
    middle_late(1, held=True)
    await_all(recv_a.at[2, :, pl.ds(EARLY, FIELDS - EARLY)], ra_sem.at[3])
    forward_late(2)
    each_peer(lambda q, _: exchange_c(1, q))
    exchange_d(0)
    middle_early(2)
    middle_late(2)
    backward(1)
    exchange_d(1)
    backward(2)
    exchange_d(2)

    decay = jnp.transpose(jnp.broadcast_to(decay_ref[...], (128, points)))
    lane1 = lax.broadcasted_iota(jnp.int32, (1, 128), 1)
    kz1 = SPAN_SCALE * ((KZB // 2) * pz + (lane1 % KZB) // 2).astype(F32)
    kz_square = kz1 * kz1
    for c in range(QUADS):
        lanes = slice(128 * c, 128 * c + 128)
        kx1 = STREAM_SCALE * ((KXB // 2) * px + c).astype(F32)
        rates = decay + visc_ref[0] * (kz_square + kx1 * kx1)
        denom = 1.0 + IMPLICIT * rates
        old[:, lanes] = (1.0 - EXPLICIT * rates) / denom * old[:, lanes]
        gain[:, lanes] = FORCING * dt_ref[0] / denom
    ready = owners * QUADS * (WALLS - 1)
    for j in range(WALLS - 1):
        await_all(recv_d.at[j], rd_sem.at[j])
    before = recv_d[: WALLS - 1].reshape(ready, 128)
    for c in range(QUADS):
        lanes, rows = slice(128 * c, 128 * c + 128), slice(c * points, (c + 1) * points)
        flux_coef[:, lanes] = dot(spread[rows, :ready], before, 1, 0)
    await_all(recv_d.at[WALLS - 1], rd_sem.at[WALLS - 1])
    last = recv_d[WALLS - 1].reshape(owners * QUADS, 128)
    solved = []
    for c in range(QUADS):
        lanes, rows = slice(128 * c, 128 * c + 128), slice(c * points, (c + 1) * points)
        new_coef = flux_coef[:, lanes] + dot(spread[rows, ready:], last, 1, 0)
        mixed = old[:, lanes] + gain[:, lanes] * new_coef
        solved.append(dot(basis_ref[...], mixed.astype(BF), 1, 0).astype(BF))
    result = dot(move[...], jnp.concatenate(solved, axis=1), 1, 1)
    out_ref[...] = result.astype(BF).reshape(out_ref.shape)

    for n, (j, lo, hi) in enumerate(pieces):
        await_all(send_a.at[j, pl.ds(0, owners - 1), pl.ds(lo, hi - lo)], sa_sem.at[n])
    for j in range(WALLS):
        await_all(recv_b.at[j, pl.ds(0, nr - 1), pl.ds(0, 2)], sb_sem.at[2 * j])
        await_all(recv_b.at[j, pl.ds(0, nr - 1), pl.ds(2, 1)], sb_sem.at[2 * j + 1])
        await_all(send_c.at[j, pl.ds(0, nr - 1)], sc_sem.at[j])
        await_all(send_d.at[j, pl.ds(0, owners - 1)], sd_sem.at[j])


def per_device(
    ng, nr, npz, tables,
    wall_vel, wall_slope, wall_curvature, vorticity, vort_slope,
    mean_profile, eigen_basis, eigen_decay, viscous_step, time_step,
):
    owners = ng * npz
    kxl = KXB * ng
    nkx, nkz = kxl * nr, KZB * npz
    nxp, nzp = nkx * 3 // 2, nkz * 3 // 2
    zb = nzp // nr
    points = WALLS * owners
    lanes = KZB * KXB
    hbm = pl.BlockSpec(memory_space=pltpu.HBM)
    vmem = pl.BlockSpec(memory_space=pltpu.VMEM)
    dma = pltpu.SemaphoreType.DMA
    scratch = [
        pltpu.VMEM((FIELDS, KZB, KXB, points), BF),
        *[pltpu.VMEM(t.shape, BF) for t in tables],
        pltpu.VMEM((points, points), BF),
        pltpu.VMEM((1, points), F32),
        pltpu.SMEM(mean_profile.shape, F32),
        pltpu.SMEM((1,), F32),
        pltpu.SMEM((1,), F32),
        pltpu.VMEM((WALLS * owners * FIELDS * QUADS, 128), F32),
        pltpu.VMEM((WALLS, owners, FIELDS, QUADS, 128), BF),
        pltpu.VMEM((WALLS, owners, FIELDS, QUADS, 128), BF),
        pltpu.VMEM((owners * EARLY * QUADS, 128), F32),
        pltpu.VMEM((QUADS, 4, owners, 128), F32),
        pltpu.VMEM((6 * kxl, nkz), BF),
        pltpu.VMEM((WALLS, 3, nzp, 2 * kxl), BF),
        pltpu.VMEM((WALLS, nr, 3, zb, 2 * kxl), BF),
        pltpu.VMEM((6, zb, nkx), BF),
        pltpu.VMEM((4, zb, nxp), F32),
        pltpu.VMEM((2, zb, nxp), BF),
        pltpu.VMEM((WALLS, nr, zb, 2 * kxl), BF),
        pltpu.VMEM((WALLS, nr, zb, 2 * kxl), BF),
        pltpu.VMEM((owners * QUADS, 128), F32),
        pltpu.VMEM((WALLS, owners, QUADS, 128), BF),
        pltpu.VMEM((WALLS, owners, QUADS, 128), BF),
        pltpu.VMEM((points, lanes), F32),
        pltpu.VMEM((points, lanes), F32),
        pltpu.VMEM((points, lanes), F32),
        pltpu.VMEM((points * QUADS, points * QUADS), BF),
        dma((FIELDS,)),
        dma((len(tables) + 5,)),
        *[dma((WALLS + 1,)) for _ in range(2)],
        *[dma((2 * WALLS,)) for _ in range(2)],
        *[dma((WALLS,)) for _ in range(4)],
    ]
    out = pl.pallas_call(
        functools.partial(kernel_body, ng, nr, npz),
        out_shape=pltpu.VMEM((lanes, points), BF),
        in_specs=[hbm] * (FIELDS + len(tables) + 5),
        out_specs=vmem,
        scratch_shapes=scratch,
        compiler_params=pltpu.CompilerParams(
            collective_id=0, has_side_effects=True, vmem_limit_bytes=60 * 1024 * 1024
        ),
    )(
        wall_slope, vorticity, wall_vel, wall_curvature, vort_slope,
        *[jnp.asarray(t) for t in tables],
        eigen_basis, eigen_decay.reshape(1, points), mean_profile, viscous_step, time_step,
    )
    return out.reshape(vorticity.shape)


def build(mesh, nr):
    npz = mesh.shape["pz"]
    ng = mesh.shape["px"] // nr
    tables = all_tables(ng, nr, npz)
    spec = P("pz", "px", None)
    return jax.shard_map(
        functools.partial(per_device, ng, nr, npz, tables),
        mesh=mesh,
        in_specs=(spec,) * 5 + (P(),) * 5,
        out_specs=spec,
        check_vma=False,
    )


def solution(mesh):
    return build(mesh, NR)
```
